32 devices in a mesh: dp: 16 (over z, y, core), tensor: 2 (over x).
Axes of the slice: x: 2, y: 2, z: 4, core: 2. Of those that a mesh axis runs over, the one named last changes fastest.
Arguments:
- tokens: bfloat16 [2, 16, 128, 2048], P(None, 'dp'), may hold values from -6 to 6
- segment_ids: int32 [2, 16, 128], P(None, 'dp'), may hold values from 0 to 3, never falling along the last dimension, each value on 1 to 64 neighbouring positions
- query_proj: bfloat16 [2048, 2048], P('dp', 'tensor'), may hold values from -0.125 to 0.125
- key_proj: bfloat16 [2048, 2048], P('dp', 'tensor'), may hold values from -0.125 to 0.125
- value_proj: bfloat16 [2048, 2048], P('dp', 'tensor'), may hold values from -0.125 to 0.125
- out_proj: bfloat16 [2048, 2048], P('dp', 'tensor'), may hold values from -0.125 to 0.125
- query_gain: float32 [2048], P('tensor'), may hold values from 0.1 to 1.9
- key_gain: float32 [2048], P('tensor'), may hold values from 0.1 to 1.9
- attn_gain: float32 [2048], replicated, may hold values from 0.1 to 1.9
- gate_proj: bfloat16 [2048, 8192], P('dp', 'tensor'), may hold values from -0.125 to 0.125
- up_proj: bfloat16 [2048, 8192], P('dp', 'tensor'), may hold values from -0.125 to 0.125
- down_proj: bfloat16 [2048, 8192], P('dp', 'tensor'), may hold values from -0.0625 to 0.0625
- mlp_gain: float32 [2048], replicated, may hold values from 0.1 to 1.9
- cotangent: bfloat16 [2, 16, 128, 2048], P(None, 'dp'), may hold values from -6 to 6
Outputs:
- layer_out: bfloat16 [2, 16, 128, 2048], P(None, 'dp')
- tokens_grad: float32 [2, 16, 128, 2048], P(None, 'dp')
- query_proj_grad: float32 [2048, 2048], P('dp', 'tensor')
- key_proj_grad: float32 [2048, 2048], P('dp', 'tensor')
- value_proj_grad: float32 [2048, 2048], P('dp', 'tensor')
- out_proj_grad: float32 [2048, 2048], P('dp', 'tensor')
- query_gain_grad: float32 [2048], P('tensor')
- key_gain_grad: float32 [2048], P('tensor')
- attn_gain_grad: float32 [2048], replicated
- gate_proj_grad: float32 [2048, 8192], P('dp', 'tensor')
- up_proj_grad: float32 [2048, 8192], P('dp', 'tensor')
- down_proj_grad: float32 [2048, 8192], P('dp', 'tensor')
- mlp_gain_grad: float32 [2048], replicated
The draws below stay inside these ranges and needn't reach their ends.
Inputs may be any that keep to these rules, and one draw needn't show every extreme that they name: `segment_ids`: along each row the segment numbers never fall; each of the 4 segments of a row has 1 to 64 tokens, and one has exactly 64.
All inputs are finite; a program needn't handle non-finite values.
Results may differ from the reference program's by a relative error of at most 0.017.
Values may be sent and summed in bfloat16 or wider, within the bound.
No kernel may reach another device: no remote copies, remote signals or barrier semaphores. Data moves between devices by JAX's collectives and lax.ppermute only.
A program may use at most 768 MiB of HBM per device.

```python
import math
import jax
import jax.numpy as jnp
import numpy as np
from jax import lax

D = 2048
HEADS = 16
HEAD_DIM = 128
FF = 8192
ROW = 128
MICRO = 2
SEQS = 4
BATCH = 16


def strengthened(result, rng, source, target, parts, factor):
    owner, partner = [(jnp.arange(result.shape[axis_at]) // (result.shape[axis_at] // parts)).reshape([-1 if axis == axis_at else 1 for axis in range(result.ndim)]) for axis_at in (source, target)]
    chosen = jax.random.permutation(rng, parts)[partner]
    strong = (owner == chosen) | (owner == (partner + parts // 2) % parts)
    return jnp.where(strong, factor * result, result)


def steps_of(own_key, extent, split, smallest, high):
    factor_of = 1.0
    for axis_at, shards_of in split:
        heights = jax.random.uniform(jax.random.fold_in(jax.random.fold_in(own_key, 6), axis_at), (shards_of,), jnp.float32, smallest / len(split), high / len(split))
        factor_of = factor_of * jnp.repeat(jnp.exp(heights), extent[axis_at] // shards_of).reshape((-1,) + (1,) * (len(extent) - 1 - axis_at))
    return factor_of


def profile(count, total, limit, slope):
    portions = [(1 << 20) // math.isqrt(standing ** slope) + 1 for standing in range(2, count + 1)]
    surplus, holding = total - limit - (count - 1), [1] * (count - 1)
    while surplus > 0:
        free = [i for i in range(count - 1) if holding[i] < limit]
        mass, budget = sum([portions[i] for i in free]), surplus
        for i in free:
            extra = min(limit - holding[i], max(1, budget * portions[i] // mass), surplus)
            holding[i] = holding[i] + extra
            surplus = surplus - extra
    return np.array([limit] + holding)


def uneven_parts(rng, number_of, total, bound, skew):
    if number_of == 2:
        one = jax.random.randint(rng, (), max(1, total - bound), min(bound, total - 1) + 1)
        return jnp.stack([one, total - one])
    lengths = jnp.asarray(profile(number_of, total, bound, skew), jnp.int32)
    twos = (number_of - 1) // 2
    source_of, taker = lengths[1:1 + 2 * twos:2], lengths[2:2 + 2 * twos:2]
    margin = jnp.minimum(source_of - 1, bound - taker)
    moved = jax.random.randint(jax.random.fold_in(rng, 1), (twos,), 0, 1 << 20) % (margin + 1)
    lengths = lengths.at[1:1 + 2 * twos:2].set(source_of - moved).at[2:2 + 2 * twos:2].set(taker + moved)
    return lengths[jax.random.permutation(jax.random.fold_in(rng, 2), number_of)]


def normal_values(key, shape, scale, reach, split=(), held_as=jnp.bfloat16):
    factor_of = steps_of(key, shape, split, -0.22, 0.18) if split else 1.0
    drawn = jax.random.normal(key, shape, jnp.float32) * scale * factor_of
    return jnp.minimum(jnp.maximum(drawn, -reach), reach).astype(held_as)


def gaussian_with(rng, dims, spread, limit, cuts, heavy, held_as=jnp.bfloat16):
    array = spread * jax.random.normal(rng, dims, jnp.float32)
    if cuts:
        array = array * steps_of(rng, dims, cuts, -0.22, 0.18)
    return jnp.clip(strengthened(array, jax.random.fold_in(rng, 3), *heavy), -limit, limit).astype(held_as)


def setup_inputs(seed: int = 0) -> dict:
    key_list = jax.random.split(jax.random.key(seed), 15)
    return {
        "tokens": gaussian_with(key_list[0], (MICRO, BATCH, ROW, D), 1.0, 6.0, ((1, 16),), (1, 3, 16, 2.0)),
        "segment_ids": jax.vmap(lambda own: jnp.searchsorted(jnp.cumsum(uneven_parts(own, SEQS, ROW, ROW // 2, 0)), jnp.arange(ROW), side="right"))(jax.random.split(key_list[1], MICRO * BATCH)).reshape((MICRO, BATCH, ROW)).astype(jnp.int32),
        "query_proj": normal_values(key_list[2], (D, D), D ** -0.5, 0.125, ((0, 16), (1, 2))),
        "key_proj": normal_values(key_list[3], (D, D), D ** -0.5, 0.125, ((0, 16), (1, 2))),
        "value_proj": normal_values(key_list[4], (D, D), D ** -0.5, 0.125, ((0, 16), (1, 2))),
        "out_proj": normal_values(key_list[5], (D, D), D ** -0.5, 0.125, ((0, 16), (1, 2))),
        "query_gain": jnp.clip(1.0 + 0.18 * jax.random.normal(key_list[6], (D,), jnp.float32), 0.1, 1.9),
        "key_gain": jnp.clip(1.0 + 0.18 * jax.random.normal(key_list[7], (D,), jnp.float32), 0.1, 1.9),
        "attn_gain": jnp.clip(1.0 + 0.18 * jax.random.normal(key_list[8], (D,), jnp.float32), 0.1, 1.9),
        "gate_proj": normal_values(key_list[9], (D, FF), D ** -0.5, 0.125, ((0, 16), (1, 2))),
        "up_proj": normal_values(key_list[10], (D, FF), D ** -0.5, 0.125, ((0, 16), (1, 2))),
        "down_proj": normal_values(key_list[11], (D, FF), FF ** -0.5, 0.0625, ((0, 16), (1, 2))),
        "mlp_gain": jnp.clip(1.0 + 0.18 * jax.random.normal(key_list[12], (D,), jnp.float32), 0.1, 1.9),
        "cotangent": gaussian_with(key_list[13], (MICRO, BATCH, ROW, D), 1.0, 6.0, ((1, 16),), (1, 3, 16, 2.0)),
    }


EPSILON = 1e-06
ROPE_BASE = 500000.0
PRECISE = lax.Precision.HIGHEST

@jax.custom_vjp
def low(v):
    return lax.optimization_barrier(v.astype(jnp.bfloat16)).astype(jnp.float32)

@jax.custom_vjp
def low_back(v):
    return v

def low_keep(v):
    return (low(v), None)

def low_pass(kept, grad):
    return (grad,)

def back_keep(v):
    return (v, None)

def back_low(kept, grad):
    return (low(grad),)
low.defvjp(low_keep, low_pass)
low_back.defvjp(back_keep, back_low)

def matmul(operand, partner):
    return jnp.dot(operand, partner, precision=PRECISE, preferred_element_type=jnp.float32)

def rms_norm(values, weights):
    return values * lax.rsqrt(lax.optimization_barrier(jnp.mean(values * values, axis=-1, keepdims=True)) + EPSILON) * weights

def positions(segment_row):
    places = jnp.arange(segment_row.shape[0], dtype=jnp.int32)
    earlier = (segment_row[None, :] == segment_row[:, None]) & (places[None, :] < places[:, None])
    return lax.optimization_barrier(jnp.sum(earlier.astype(jnp.int32), axis=1)).astype(jnp.int32)

def rotary(values, places):
    row_count, row_width = values.shape
    per_head = values.reshape(row_count, row_width // HEAD_DIM, HEAD_DIM)
    halfway = HEAD_DIM // 2
    inverse = jnp.exp(jnp.arange(halfway, dtype=jnp.float32) * (-2.0 * math.log(ROPE_BASE) / HEAD_DIM))
    angles = places.astype(jnp.float32)[:, None] * inverse[None, :]
    cosine = jnp.cos(angles)[:, None, :]
    sine_table = jnp.sin(angles)[:, None, :]
    leading = per_head[..., :halfway]
    trailing = per_head[..., halfway:]
    turned = jnp.concatenate([leading * cosine - trailing * sine_table, trailing * cosine + leading * sine_table], axis=-1)
    return turned.reshape(row_count, row_width)

def layer_forward(tokens_row, query_proj, key_proj, value_proj, out_proj, query_gain, key_gain, attn_gain, gate_proj, up_proj, down_proj, mlp_gain, segment_row):
    row_count = tokens_row.shape[0]
    places = positions(segment_row)
    indices = jnp.arange(row_count, dtype=jnp.int32)
    queries = low_back(matmul(tokens_row, query_proj))
    keyed = low_back(matmul(tokens_row, key_proj))
    valued = low(low_back(matmul(tokens_row, value_proj)))
    query_rot = low(rotary(rms_norm(queries, query_gain), places))
    key_rot = low(rotary(rms_norm(keyed, key_gain), places))
    query_heads = query_rot.reshape(row_count, HEADS, HEAD_DIM)
    key_heads = key_rot.reshape(row_count, HEADS, HEAD_DIM)
    value_heads = valued.reshape(row_count, HEADS, HEAD_DIM)
    scores = low_back(jnp.einsum('qhd,khd->hqk', query_heads, key_heads, precision=PRECISE)) * HEAD_DIM ** (-0.5)
    allowed = (segment_row[None, :] == segment_row[:, None]) & (indices[None, :] <= indices[:, None])
    scores = jnp.where(allowed[None], scores, -1e+30)
    highest = lax.optimization_barrier(jnp.max(scores, axis=-1, keepdims=True))
    expo = jnp.exp(scores - highest)
    probs = expo / lax.optimization_barrier(jnp.sum(expo, axis=-1, keepdims=True))
    mixed = jnp.einsum('hqk,khd->qhd', low(probs), value_heads, precision=PRECISE)
    mixed = low(low_back(mixed.reshape(row_count, D)))
    projected = low_back(matmul(mixed, out_proj.T))
    hidden = tokens_row + rms_norm(projected, attn_gain)
    hidden_low = low(hidden)
    gated = low_back(matmul(hidden_low, gate_proj))
    lifted = low_back(matmul(hidden_low, up_proj))
    active = low(gated / (1.0 + jnp.exp(-gated)) * lifted)
    reduced = low_back(matmul(active, down_proj.T))
    return hidden + rms_norm(reduced, mlp_gain)

def reference(tokens, segment_ids, query_proj, key_proj, value_proj, out_proj, query_gain, key_gain, attn_gain, gate_proj, up_proj, down_proj, mlp_gain, cotangent):
    weights = tuple((matrix.astype(jnp.float32) for matrix in (query_proj, key_proj, value_proj, out_proj, query_gain, key_gain, attn_gain, gate_proj, up_proj, down_proj, mlp_gain)))
    inputs = tokens.astype(jnp.float32).reshape(-1, ROW, D)
    segment_rows = segment_ids.reshape(-1, ROW).astype(jnp.int32)
    pulled = cotangent.astype(jnp.float32).reshape(-1, ROW, D)

    def one_row(totals, row_item):
        tokens_row, segment_row, cotangent_row = row_item

        def forward(inputs_row, *params):
            return layer_forward(inputs_row, *params, segment_row)
        output, backward = jax.vjp(forward, tokens_row, *weights)
        gradients = backward(cotangent_row)
        totals = tuple((running + addend for running, addend in zip(totals, gradients[1:])))
        return (totals, (output.astype(jnp.bfloat16), gradients[0]))
    start = tuple((jnp.zeros(matrix.shape, jnp.float32) for matrix in weights))
    totals, (outputs, input_grads) = lax.scan(one_row, start, (inputs, segment_rows, pulled))
    full_shape = tokens.shape
    return (outputs.reshape(full_shape), input_grads.reshape(full_shape), totals[0], totals[1], totals[2], totals[3], totals[4], totals[5], totals[6], totals[7], totals[8], totals[9], totals[10])
```

```python
import math

import jax
import jax.numpy as jnp
from jax import lax
from jax.sharding import Mesh, PartitionSpec as P

D = 2048
HEAD_DIM = 128
EPSILON = 1e-06
ROPE_BASE = 500000.0
GROUP = 4
CORES = 2
F32 = jnp.float32
BF16 = jnp.bfloat16
TEAM = ("g", "c")


def dot(a, b):
    return jnp.dot(a, b, preferred_element_type=F32)


def dot_nt(a, b):
    return lax.dot_general(a, b, (((1,), (1,)), ((), ())), preferred_element_type=F32)


def dot_tn(a, b):
    return lax.dot_general(a, b, (((0,), (0,)), ((), ())), preferred_element_type=F32)


def swap(value, axis):
    return lax.ppermute(value, axis, [(0, 1), (1, 0)])


def shift(value, by):
    return lax.ppermute(value, "g", [(i, (i + by) % GROUP) for i in range(GROUP)])


def pick(value, index, axis):
    return lax.dynamic_index_in_dim(value, index, axis, keepdims=False)


def put(value, piece, index, axis=0):
    return lax.dynamic_update_index_in_dim(value, piece, index, axis)


def ordered(flag, first, second, axis):
    return jnp.where(
        flag == 0, jnp.stack([first, second], axis), jnp.stack([second, first], axis)
    )


class Place:
    def __init__(self, reps):
        self.reps = reps
        self.g = lax.axis_index("g")
        self.q = lax.axis_index("q")
        self.c = lax.axis_index("c")
        self.x = lax.axis_index("x")

    def to_local(self, value):
        lead = value.shape[:-1]
        value = value.reshape(lead + (GROUP, self.reps, D // (GROUP * self.reps)))
        value = jnp.swapaxes(value, -3, -2)
        if self.reps == 2:
            value = jnp.where(self.q == 0, value, jnp.flip(value, -3))
        return value.reshape(lead + (D,))

    def to_global(self, value):
        lead = value.shape[:-1]
        value = value.reshape(lead + (self.reps, GROUP, D // (GROUP * self.reps)))
        if self.reps == 2:
            value = jnp.where(self.q == 0, value, jnp.flip(value, -3))
        return jnp.swapaxes(value, -3, -2).reshape(lead + (D,))

    def spread(self, shard):
        rows, _, width = shard.shape
        shard = shard.reshape(rows, GROUP, CORES, width)
        mine = pick(shard, self.c, 2)
        got = swap(pick(shard, 1 - self.c, 2), "c")
        both = ordered(self.c, mine, got, 0)
        held = jnp.zeros((GROUP, CORES, rows, width), shard.dtype)
        for by in range(GROUP):
            piece = pick(both, (self.g + by) % GROUP, 2)
            if by:
                piece = shift(piece, by)
            held = put(held, piece, (self.g - by) % GROUP)
        return held.reshape(GROUP * CORES * rows, width)

    def widen(self, held):
        if self.reps != 2:
            tall = lax.all_gather(held, "q", axis=0, tiled=True)
            return tall, swap(tall, "x")
        half = held.shape[0] // 2
        beside = swap(held, "x")
        below = swap(held, "q")
        corner_top = swap(beside[:half], "q")
        corner_low = swap(below[half:], "x")
        return (
            jnp.concatenate([held, below], 0),
            jnp.concatenate([beside, corner_top, corner_low], 0),
        )

    def narrow(self, own, other):
        if self.reps != 2:
            own = own + swap(other, "x")
            return lax.psum_scatter(own, "q", scatter_dimension=0, tiled=True)
        size = own.shape[0] // 2
        half = size // 2
        keep, below = own[:size], own[size:]
        beside, corner = other[:size], other[size:]
        add = lambda a, b: (a.astype(F32) + b.astype(F32)).astype(BF16)
        top = swap(corner[:half], "q")
        low = swap(corner[half:], "x")
        beside = jnp.concatenate([add(beside[:half], top), beside[half:]], 0)
        below = jnp.concatenate([below[:half], add(below[half:], low)], 0)
        from_x = swap(beside, "x")
        from_q = swap(below, "q")
        return (keep.astype(F32) + from_x.astype(F32) + from_q.astype(F32)).astype(BF16)

    def collect(self, held):
        width = held.shape[1]
        held = held.reshape(GROUP, CORES, -1, width)
        slots = jnp.zeros_like(held)
        for by in range(GROUP):
            piece = pick(held, (self.g + by) % GROUP, 0)
            if by:
                piece = shift(piece, by)
            slots = put(slots, piece, (self.g - by) % GROUP)
        mine = pick(slots, self.c, 1)
        got = swap(pick(slots, 1 - self.c, 1), "c")
        both = ordered(self.c, mine, got, 1)
        return both.reshape(GROUP * CORES, -1, width)

    def team_sum(self, value):
        value = value + swap(value, "c")
        for step in (1, 2):
            value = value + lax.ppermute(value, "g", [(i, i ^ step) for i in range(GROUP)])
        return value

    def total(self, value):
        value = self.team_sum(value)
        value = value + swap(value, "x")
        return value + swap(value, "q") if self.reps == 2 else lax.psum(value, "q")


def rope_tables(segments):
    places = jnp.arange(segments.shape[1], dtype=jnp.int32)
    same = segments[:, :, None] == segments[:, None, :]
    earlier = same & (places[None, None, :] < places[None, :, None])
    allowed = same & (places[None, None, :] <= places[None, :, None])
    spot = jnp.sum(earlier.astype(jnp.int32), axis=2).astype(F32)
    halfway = HEAD_DIM // 2
    inverse = jnp.exp(jnp.arange(halfway, dtype=F32) * (-2.0 * math.log(ROPE_BASE) / HEAD_DIM))
    angles = spot[:, :, None] * inverse
    return allowed, jnp.cos(angles), jnp.sin(angles)


def turn(values, cosine, sine):
    halfway = HEAD_DIM // 2
    a, b = values[..., :halfway], values[..., halfway:]
    cosine, sine = cosine[:, :, None], sine[:, :, None]
    return jnp.concatenate([a * cosine - b * sine, b * cosine + a * sine], -1)


def norm_scale(values):
    return lax.rsqrt(jnp.mean(values * values, axis=-1, keepdims=True) + EPSILON)


def norm_back(values, scale, gain, grad):
    weighted = grad * gain
    inner = jnp.sum(values * weighted, axis=-1, keepdims=True) / D
    return (
        scale * weighted - values * (scale * scale * scale) * inner,
        jnp.sum(grad * values * scale, axis=0),
    )


def on_device(
    reps,
    tokens,
    segment_ids,
    query_proj,
    key_proj,
    value_proj,
    out_proj,
    query_gain,
    key_gain,
    attn_gain,
    gate_proj,
    up_proj,
    down_proj,
    mlp_gain,
    cotangent,
):
    place = Place(reps)
    slots = GROUP * CORES
    shard_rows = query_proj.shape[0]
    length = tokens.shape[2]
    slot = place.g * CORES + place.c

    own_row = place.to_local(pick(tokens, place.x, 0)[0])
    own_cotangent = place.to_local(pick(cotangent, place.x, 0)[0]).astype(F32)
    attn_gain = place.to_local(attn_gain)
    mlp_gain = place.to_local(mlp_gain)

    by_slot = lambda w: w.reshape(shard_rows, slots, -1)
    attn_shard = jnp.concatenate(
        [by_slot(w) for w in (query_proj, key_proj, value_proj, out_proj)], axis=2
    )
    attn_held = place.spread(attn_shard)
    all_rows = lax.all_gather(own_row, TEAM, axis=0, tiled=True)

    segments = pick(segment_ids, place.x, 0)
    segments = ordered(place.c, segments, swap(segments, "c"), 0)[:, 0]
    gathered = jnp.zeros((GROUP,) + segments.shape, segments.dtype)
    for by in range(GROUP):
        piece = shift(segments, by) if by else segments
        gathered = put(gathered, piece, (place.g - by) % GROUP)
    segments = gathered.reshape(slots, length)
    allowed, cosine, sine = rope_tables(segments)

    gains = jnp.stack([pick(w.reshape(slots, HEAD_DIM), slot, 0) for w in (query_gain, key_gain)])
    gains = jnp.stack([gains, swap(gains, "x")], 1)

    attn_own, attn_other = place.widen(attn_held)
    gate_full = jnp.concatenate(place.widen(place.spread(by_slot(gate_proj))), 1)
    up_full = jnp.concatenate(place.widen(place.spread(by_slot(up_proj))), 1)
    down_full = jnp.concatenate(place.widen(place.spread(by_slot(down_proj))), 1)

    cut = 3 * HEAD_DIM
    qkv_full = jnp.concatenate([attn_own[:, :cut], attn_other[:, :cut]], 1)
    out_full = jnp.concatenate([attn_own[:, cut:], attn_other[:, cut:]], 1)

    qkv = dot(all_rows, qkv_full).reshape(slots, length, 2, 3, HEAD_DIM)
    queries, keyed, value_low = qkv[:, :, :, 0], qkv[:, :, :, 1], qkv[:, :, :, 2].astype(BF16)
    squares = jnp.stack(
        [jnp.sum(queries * queries, axis=(2, 3)), jnp.sum(keyed * keyed, axis=(2, 3))]
    )
    scales = lax.rsqrt(place.team_sum(squares) / D + EPSILON)[:, :, :, None, None]
    query_low = turn(queries * scales[0] * gains[0], cosine, sine).astype(BF16)
    key_low = turn(keyed * scales[1] * gains[1], cosine, sine).astype(BF16)

    def einsum(spec, a, b):
        return jnp.einsum(spec, a, b, preferred_element_type=F32)

    root = HEAD_DIM ** (-0.5)
    scores = einsum("bqhd,bkhd->bhqk", query_low, key_low) * root
    scores = jnp.where(allowed[:, None], scores, -1e30)
    expo = jnp.exp(scores - jnp.max(scores, axis=-1, keepdims=True))
    probs = expo / jnp.sum(expo, axis=-1, keepdims=True)
    probs_low = probs.astype(BF16)
    mixed = einsum("bhqk,bkhd->bqhd", probs_low, value_low).astype(BF16)
    mixed = mixed.reshape(slots * length, 2 * HEAD_DIM)

    def team_scatter(value):
        return lax.psum_scatter(
            value.astype(BF16), TEAM, scatter_dimension=0, tiled=True
        ).astype(F32)

    def team_gather(value):
        return lax.all_gather(value, TEAM, axis=0, tiled=True)

    projected = team_scatter(dot_nt(mixed, out_full))
    projected_scale = norm_scale(projected)
    hidden = own_row.astype(F32) + projected * projected_scale * attn_gain
    hidden_all = team_gather(hidden.astype(BF16))
    lifted = dot(hidden_all, up_full)
    gated = dot(hidden_all, gate_full)
    active = (gated / (1.0 + jnp.exp(-gated)) * lifted).astype(BF16)
    reduced = team_scatter(dot_nt(active, down_full))
    reduced_scale = norm_scale(reduced)

    reduced_grad, mlp_gain_grad = norm_back(reduced, reduced_scale, mlp_gain, own_cotangent)
    reduced_all = team_gather(reduced_grad.astype(BF16))
    own_out = place.to_global((hidden + reduced * reduced_scale * mlp_gain).astype(BF16))
    layer_out = ordered(place.x, own_out, swap(own_out, "x"), 0)[:, None]

    active_grad = dot(reduced_all, down_full)
    gate_sigmoid = 1.0 / (1.0 + jnp.exp(-gated))
    gated_grad = (active_grad * lifted * gate_sigmoid * (1.0 + gated * (1.0 - gate_sigmoid))).astype(
        BF16
    )
    lifted_grad = (active_grad * gated * gate_sigmoid).astype(BF16)
    hidden_grad = own_cotangent + team_scatter(
        dot_nt(gated_grad, gate_full) + dot_nt(lifted_grad, up_full)
    )
    projected_grad, attn_gain_grad = norm_back(projected, projected_scale, attn_gain, hidden_grad)
    projected_all = team_gather(projected_grad.astype(BF16))

    def send_grad(grad):
        width = grad.shape[1] // 2
        low = grad.astype(BF16)
        return place.collect(place.narrow(low[:, :width], low[:, width:]))

    down_grad = send_grad(dot_tn(reduced_all, active))
    gate_grad = send_grad(dot_tn(hidden_all, gated_grad))
    up_grad = send_grad(dot_tn(hidden_all, lifted_grad))

    mixed_grad = dot(projected_all, out_full).astype(BF16)
    mixed_grad = mixed_grad.reshape(slots, length, 2, HEAD_DIM)
    value_grad = einsum("bhqk,bqhd->bkhd", probs_low, mixed_grad)
    prob_grad = einsum("bqhd,bkhd->bhqk", mixed_grad, value_low)
    score_grad = (
        probs * (prob_grad - jnp.sum(probs * prob_grad, axis=-1, keepdims=True)) * root
    ).astype(BF16)
    query_normed_grad = turn(einsum("bhqk,bkhd->bqhd", score_grad, key_low), cosine, -sine)
    key_normed_grad = turn(einsum("bhqk,bqhd->bkhd", score_grad, query_low), cosine, -sine)
    query_weighted = query_normed_grad * gains[0]
    key_weighted = key_normed_grad * gains[1]
    inner = jnp.stack(
        [jnp.sum(queries * query_weighted, axis=(2, 3)), jnp.sum(keyed * key_weighted, axis=(2, 3))]
    )
    inner = place.team_sum(inner)[:, :, :, None, None] / D
    query_grad = scales[0] * query_weighted - queries * scales[0] ** 3 * inner[0]
    key_grad = scales[1] * key_weighted - keyed * scales[1] ** 3 * inner[1]
    qkv_grad = jnp.stack([query_grad, key_grad, value_grad], 3).astype(BF16)
    qkv_grad = qkv_grad.reshape(slots * length, 6 * HEAD_DIM)

    input_grad = hidden_grad + team_scatter(dot_nt(qkv_grad, qkv_full))
    own_grad = place.to_global(input_grad.astype(BF16))
    tokens_grad = ordered(place.x, own_grad, swap(own_grad, "x"), 0)[:, None].astype(F32)

    qkv_weight_grad = dot_tn(all_rows, qkv_grad).astype(BF16)
    out_weight_grad = dot_tn(projected_all, mixed).astype(BF16)
    attn_grad = place.collect(
        place.narrow(
            jnp.concatenate([qkv_weight_grad[:, :cut], out_weight_grad[:, :HEAD_DIM]], 1),
            jnp.concatenate([qkv_weight_grad[:, cut:], out_weight_grad[:, HEAD_DIM:]], 1),
        )
    )

    head_gain_grads = jnp.stack(
        [
            jnp.sum(query_normed_grad * queries * scales[0], axis=(0, 1)),
            jnp.sum(key_normed_grad * keyed * scales[1], axis=(0, 1)),
        ]
    )
    spots = jnp.zeros((2, 2, slots, HEAD_DIM), F32)
    for head in range(2):
        spots = lax.dynamic_update_slice(
            spots,
            head_gain_grads[:, head][:, None, None],
            (0, place.x if head == 0 else 1 - place.x, slot, 0),
        )
    summed = place.total(
        jnp.concatenate(
            [
                spots.reshape(2, D),
                place.to_global(attn_gain_grad)[None],
                place.to_global(mlp_gain_grad)[None],
            ]
        )
    )
    half_of = lambda v: pick(v.reshape(2, -1), place.x, 0)

    def unslot(grad):
        return jnp.swapaxes(grad, 0, 1).reshape(shard_rows, -1).astype(F32)

    return (
        layer_out,
        tokens_grad,
        *[unslot(attn_grad[:, :, i * HEAD_DIM : (i + 1) * HEAD_DIM]) for i in range(4)],
        half_of(summed[0]),
        half_of(summed[1]),
        summed[2],
        unslot(gate_grad),
        unslot(up_grad),
        unslot(down_grad),
        summed[3],
    )


def solution(mesh):
    reps = mesh.shape["dp"] // (GROUP * CORES)
    folded = Mesh(
        mesh.devices.reshape(GROUP, reps, CORES, mesh.shape["tensor"]), ("g", "q", "c", "x")
    )
    dp = ("g", "q", "c")
    row = P(None, dp, None, None)
    weight = P(dp, "x")
    gain = P("x")
    in_specs = (row, P(None, dp, None)) + (weight,) * 4 + (gain, gain, P()) + (weight,) * 3
    in_specs += (P(), row)
    out_specs = (row, row) + (weight,) * 4 + (gain, gain, P()) + (weight,) * 3 + (P(),)

    def body(*args):
        return on_device(reps, *args)

    return jax.shard_map(
        body, mesh=folded, in_specs=in_specs, out_specs=out_specs, check_vma=False
    )
```

```python
import math

import jax
import jax.numpy as jnp
from jax import lax
from jax.experimental import pallas as pl
from jax.experimental.pallas import tpu as pltpu
from jax.sharding import Mesh, PartitionSpec as P

D = 2048
HEAD_DIM = 128
EPSILON = 1e-06
ROPE_BASE = 500000.0
GROUP = 4
CORES = 2
F32 = jnp.float32
BF16 = jnp.bfloat16
TEAM = ("g", "c")


def dot(a, b):
    return jnp.dot(a, b, preferred_element_type=F32)


def dot_nt(a, b):
    return lax.dot_general(a, b, (((1,), (1,)), ((), ())), preferred_element_type=F32)


def dot_tn(a, b):
    return lax.dot_general(a, b, (((0,), (0,)), ((), ())), preferred_element_type=F32)


def swap(value, axis):
    return lax.ppermute(value, axis, [(0, 1), (1, 0)])


def shift(value, by):
    return lax.ppermute(value, "g", [(i, (i + by) % GROUP) for i in range(GROUP)])


def pick(value, index, axis):
    return lax.dynamic_index_in_dim(value, index, axis, keepdims=False)


def put(value, piece, index, axis=0):
    return lax.dynamic_update_index_in_dim(value, piece, index, axis)


def ordered(flag, first, second, axis):
    return jnp.where(
        flag == 0, jnp.stack([first, second], axis), jnp.stack([second, first], axis)
    )


def add(*values):
    return sum(v.astype(F32) for v in values).astype(BF16)


class Order:
    def __init__(self):
        self.token = jnp.zeros((), F32)

    def __call__(self, *values):
        *values, self.token = lax.optimization_barrier((*values, self.token))
        return values[0] if len(values) == 1 else values


def assemble(pieces, moves, shapes):
    def kernel(*refs):
        sources, (*targets, sems) = refs[: len(pieces)], refs[len(pieces) :]
        copies = []
        for number, (source, columns, target, row, column) in enumerate(moves):
            rows, width = pieces[source].shape[0], columns[1] - columns[0]
            copies.append(
                pltpu.make_async_copy(
                    sources[source].at[:, pl.ds(columns[0], width)],
                    targets[target].at[pl.ds(row, rows), pl.ds(column, width)],
                    sems.at[number],
                )
            )
        for copy in copies:
            copy.start()
        for copy in copies:
            copy.wait()

    out = pl.pallas_call(
        kernel,
        out_shape=[jax.ShapeDtypeStruct(shape, pieces[0].dtype) for shape in shapes],
        in_specs=[pl.BlockSpec(memory_space=pl.ANY)] * len(pieces),
        out_specs=[pl.BlockSpec(memory_space=pltpu.VMEM)] * len(shapes),
        scratch_shapes=[pltpu.SemaphoreType.DMA((len(moves),))],
        compiler_params=pltpu.CompilerParams(vmem_limit_bytes=24 << 20),
        cost_estimate=pl.CostEstimate(
            flops=0,
            bytes_accessed=sum(4 * math.prod(shape) for shape in shapes),
            transcendentals=0,
        ),
    )(*pieces)
    return out


def reorder(values, flag, orders):
    size = values.shape[1] // len(orders[0])

    def kernel(flag_ref, source, target):
        for number, order in enumerate(orders):

            @pl.when(flag_ref[0] == number)
            def _():
                for to, block in enumerate(order):
                    target[:, to * size : (to + 1) * size] = source[
                        :, block * size : (block + 1) * size
                    ]

    return pl.pallas_call(
        kernel,
        out_shape=jax.ShapeDtypeStruct(values.shape, values.dtype),
        in_specs=[
            pl.BlockSpec(memory_space=pltpu.SMEM),
            pl.BlockSpec(memory_space=pltpu.VMEM),
        ],
        out_specs=pl.BlockSpec(memory_space=pltpu.VMEM),
        cost_estimate=pl.CostEstimate(
            flops=0, bytes_accessed=4 * values.size, transcendentals=0
        ),
    )(jnp.reshape(flag, (1,)).astype(jnp.int32), values)


def vmem_call(kernel, shapes, scalars, arrays):
    flags = jnp.stack([jnp.asarray(v, jnp.int32) for v in scalars])
    spec = pl.BlockSpec(memory_space=pltpu.VMEM)
    return pl.pallas_call(
        kernel,
        out_shape=shapes,
        in_specs=[pl.BlockSpec(memory_space=pltpu.SMEM)] + [spec] * len(arrays),
        out_specs=[spec] * len(shapes),
        compiler_params=pltpu.CompilerParams(vmem_limit_bytes=VMEM_LIMIT),
        cost_estimate=pl.CostEstimate(flops=0, bytes_accessed=LOCAL_BYTES, transcendentals=0),
    )(flags, *arrays)


def pack(shards, g):
    rows, width = shards[0].shape[0], shards[0].shape[1] // (GROUP * CORES)
    count = len(shards)

    def kernel(flags, *refs):
        sources, targets = refs[:count], refs[count:]
        for by in range(GROUP):
            to = lax.rem(flags[0] + by, GROUP)
            for core in range(CORES):
                start = pl.multiple_of((to * CORES + core) * width, width)
                for number in range(count):
                    at = (core * count + number) * width
                    targets[by][:, at : at + width] = sources[number][:, pl.ds(start, width)]

    shape = jax.ShapeDtypeStruct((rows, CORES * count * width), shards[0].dtype)
    return vmem_call(kernel, [shape] * GROUP, [g], shards)


def sort(pieces, g, c):
    rows, half = pieces[0].shape[0], pieces[0].shape[1] // CORES

    def kernel(flags, *refs):
        sources, targets = refs[:GROUP], refs[GROUP:]
        for by in range(GROUP):
            row = pl.multiple_of(lax.rem(flags[0] + GROUP - by, GROUP) * rows, rows)
            for number in range(CORES):
                core = flags[1] if number == 0 else 1 - flags[1]
                targets[number][pl.ds(row, rows), :] = sources[by][
                    :, pl.ds(pl.multiple_of(core * half, half), half)
                ]

    shape = jax.ShapeDtypeStruct((GROUP * rows, half), pieces[0].dtype)
    return vmem_call(kernel, [shape] * CORES, [g, c], pieces)


def unpack(pieces, g, count):
    rows, width = pieces[0].shape[0], pieces[0].shape[1] // (CORES * count)

    def kernel(flags, *refs):
        sources, targets = refs[:GROUP], refs[GROUP:]
        for by in range(GROUP):
            source = lax.rem(flags[0] + GROUP - by, GROUP)
            for core in range(CORES):
                start = pl.multiple_of((source * CORES + core) * width, width)
                for number in range(count):
                    at = (core * count + number) * width
                    targets[number][:, pl.ds(start, width)] = sources[by][
                        :, at : at + width
                    ].astype(F32)

    shape = jax.ShapeDtypeStruct((rows, GROUP * CORES * width), F32)
    return vmem_call(kernel, [shape] * count, [g], pieces)


def by_core(mine, got, c):
    rows = mine.shape[0]

    def kernel(flags, first, second, target):
        target[pl.ds(pl.multiple_of(flags[0] * rows, rows), rows), :] = first[...]
        target[pl.ds(pl.multiple_of((1 - flags[0]) * rows, rows), rows), :] = second[...]

    [out] = vmem_call(
        kernel,
        [jax.ShapeDtypeStruct((CORES * rows, mine.shape[1]), mine.dtype)],
        [c],
        [mine, got],
    )
    return out


def deal(mine, got, g, c):
    rows, width = mine.shape[0] // GROUP, mine.shape[1]

    def kernel(flags, first, second, *targets):
        for by in range(GROUP):
            row = pl.multiple_of(lax.rem(flags[0] + by, GROUP) * rows, rows)
            for number, source in enumerate((first, second)):
                core = flags[1] if number == 0 else 1 - flags[1]
                at = pl.ds(pl.multiple_of(core * width, width), width)
                targets[by][:, at] = source[pl.ds(row, rows), :]

    shape = jax.ShapeDtypeStruct((rows, CORES * width), mine.dtype)
    return vmem_call(kernel, [shape] * GROUP, [g, c], [mine, got])


def weight_grads(factors, reps, cuts):
    step = 256
    count = factors[0][0].shape[0]
    total = sum(cuts)
    starts = [sum(cuts[:number]) for number in range(len(cuts))]

    def products(lefts, rights, own, other):
        for left, right, start, width in zip(lefts, rights, starts, cuts):
            product = mm(left[...], right[...], TN).astype(BF16)
            own[:, start : start + width] = product[:, :width]
            other[:, start : start + width] = product[:, width:]

    lefts = [left for left, _ in factors]
    rights = [right for _, right in factors]
    size = len(factors)
    whole = [pl.BlockSpec(v.shape, lambda i: (0, 0)) for v in rights]
    params = {
        "compiler_params": pltpu.CompilerParams(vmem_limit_bytes=VMEM_LIMIT),
        "cost_estimate": pl.CostEstimate(flops=0, bytes_accessed=LOCAL_BYTES, transcendentals=0),
    }
    if reps != 2:

        def kernel(*refs):
            products(refs[:size], refs[size : 2 * size], *refs[2 * size :])

        out = pl.BlockSpec((step, total), lambda i: (i, 0))
        return pl.pallas_call(
            kernel,
            grid=(D // step,),
            in_specs=[pl.BlockSpec((count, step), lambda i: (0, i))] * size + whole,
            out_specs=[out, out],
            out_shape=[jax.ShapeDtypeStruct((D, total), BF16)] * 2,
            **params,
        )(*lefts, *rights)

    steps = D // 2 // step
    half = steps // 2

    def kernel(*refs):
        upper, lower, right = refs[:size], refs[size : 2 * size], refs[2 * size : 3 * size]
        to_q, to_x, beside_top, below_low, keep = refs[3 * size :]

        @pl.when(pl.program_id(0) < half)
        def _():
            products(upper, right, keep, beside_top)
            products(lower, right, to_q.at[1], to_q.at[0])

        @pl.when(pl.program_id(0) >= half)
        def _():
            products(upper, right, keep, to_x.at[1])
            products(lower, right, below_low, to_x.at[0])

    first = lambda i: jnp.minimum(i, half - 1)
    last = lambda i: jnp.maximum(i - half, 0)
    rows = D // 4
    return pl.pallas_call(
        kernel,
        grid=(steps,),
        in_specs=[pl.BlockSpec((count, step), lambda i: (0, i))] * size
        + [pl.BlockSpec((count, step), lambda i: (0, i + steps))] * size
        + whole,
        out_specs=[
            pl.BlockSpec((2, step, total), lambda i: (0, first(i), 0)),
            pl.BlockSpec((2, step, total), lambda i: (0, last(i), 0)),
            pl.BlockSpec((step, total), lambda i: (first(i), 0)),
            pl.BlockSpec((step, total), lambda i: (last(i), 0)),
            pl.BlockSpec((step, total), lambda i: (i, 0)),
        ],
        out_shape=[
            jax.ShapeDtypeStruct(shape, BF16)
            for shape in (
                (2, rows, total), (2, rows, total), (rows, total), (rows, total), (2 * rows, total)
            )
        ],
        **params,
    )(*lefts, *lefts, *rights)


NN, NT, TN = ((1,), (0,)), ((1,), (1,)), ((0,), (0,))
VMEM_LIMIT = 60 << 20
LOCAL_BYTES = 200 << 20
HEADS_HERE = 2
ROOT = HEAD_DIM ** (-0.5)


def mm(a, b, dims=NN):
    return lax.dot_general(a, b, (dims, ((), ())), preferred_element_type=F32)


def eye(size):
    return lax.broadcasted_iota(jnp.int32, (size, size), 0) == lax.broadcasted_iota(
        jnp.int32, (size, size), 1
    )


def to_column(row):
    return jnp.sum(jnp.where(eye(row.shape[1]), row, 0.0), axis=1, keepdims=True)


def to_row(column):
    return jnp.sum(jnp.where(eye(column.shape[0]), column, 0.0), axis=0, keepdims=True)


def head(values, kind, number):
    start = (number * 3 + kind) * HEAD_DIM
    return values[:, start : start + HEAD_DIM]


def pair(values, number):
    return values[:, number * HEAD_DIM : (number + 1) * HEAD_DIM]


def rotated(values, cosine, sine):
    return values * cosine + pltpu.roll(values, HEAD_DIM // 2, 1) * sine


def allowed_keys(segment_row):
    size = segment_row.shape[1]
    same = to_column(segment_row) == segment_row
    later = lax.broadcasted_iota(jnp.int32, (size, size), 1) > lax.broadcasted_iota(
        jnp.int32, (size, size), 0
    )
    return jnp.logical_and(same, jnp.logical_not(later))


def softmax_of(query, key, allowed):
    scores = jnp.where(allowed, mm(query, key, NT) * ROOT, -1e30)
    expo = jnp.exp(scores - jnp.max(scores, axis=1, keepdims=True))
    return expo / jnp.sum(expo, axis=1, keepdims=True)


def scale_of(squares, kind):
    return to_column(lax.rsqrt(squares[kind : kind + 1] / D + EPSILON))


def row_call(kernel, rows, ins, outs):
    def spec(shape, block):
        if block == "whole":
            return pl.BlockSpec(shape, lambda i: (0,) * len(shape))
        return pl.BlockSpec((block,) + shape[1:], lambda i: (i,) + (0,) * (len(shape) - 1))

    return pl.pallas_call(
        kernel,
        grid=(rows,),
        in_specs=[spec(v.shape, block) for v, block in ins],
        out_specs=[spec(shape, block) for shape, _, block in outs],
        out_shape=[jax.ShapeDtypeStruct(shape, dtype) for shape, dtype, _ in outs],
        compiler_params=pltpu.CompilerParams(vmem_limit_bytes=VMEM_LIMIT),
        cost_estimate=pl.CostEstimate(flops=0, bytes_accessed=0, transcendentals=0),
    )(*[v for v, _ in ins])


def project_kernel(tokens, weights, out, squares):
    product = mm(tokens[...], weights[...])
    out[...] = product
    for kind in range(2):
        total = 0.0
        for number in range(HEADS_HERE):
            part = head(product, kind, number)
            total = total + jnp.sum(part * part, axis=1, keepdims=True)
        squares[0, kind : kind + 1] = to_row(total)


def attend_kernel(
    qkv, squares, gains, cosine, sine, segments, weights, query_out, key_out, value_out, mixed, out
):
    allowed = allowed_keys(segments[0])
    scales = [scale_of(squares[0], kind) for kind in range(2)]
    for number in range(HEADS_HERE):
        low = [
            rotated(
                head(qkv, kind, number) * scales[kind] * gains[kind, number : number + 1],
                cosine[...],
                sine[...],
            ).astype(BF16)
            for kind in range(2)
        ]
        value = head(qkv, 2, number).astype(BF16)
        probs = softmax_of(*low, allowed).astype(BF16)
        where = slice(number * HEAD_DIM, (number + 1) * HEAD_DIM)
        query_out[:, where] = low[0]
        key_out[:, where] = low[1]
        value_out[:, where] = value
        mixed[:, where] = mm(probs, value).astype(BF16)
    out[...] = mm(mixed[...], weights[...], NT).astype(BF16)


def attend_back_kernel(
    grads, weights, queries, keys, values, qkv, squares, gains, cosine, sine, segments,
    weighted, value_grad, inner, gain_grad,
):
    @pl.when(pl.program_id(0) == 0)
    def _():
        gain_grad[...] = jnp.zeros_like(gain_grad)

    allowed = allowed_keys(segments[0])
    scales = [scale_of(squares[0], kind) for kind in range(2)]
    mixed_grads = mm(grads[...], weights[...]).astype(BF16)
    sums = [0.0, 0.0]
    for number in range(HEADS_HERE):
        query, key, value = pair(queries, number), pair(keys, number), pair(values, number)
        mixed_grad = pair(mixed_grads, number)
        probs = softmax_of(query, key, allowed)
        where = slice(number * HEAD_DIM, (number + 1) * HEAD_DIM)
        value_grad[:, where] = mm(probs.astype(BF16), mixed_grad, TN).astype(BF16)
        prob_grad = mm(mixed_grad, value, NT)
        score_grad = probs * (prob_grad - jnp.sum(probs * prob_grad, axis=1, keepdims=True))
        score_low = (score_grad * ROOT).astype(BF16)
        turned = (mm(score_low, key), mm(score_low, query, TN))
        for kind in range(2):
            normed = rotated(turned[kind], cosine[...], -sine[...])
            part = head(qkv, kind, number)
            gain_grad[kind, number : number + 1] += jnp.sum(
                normed * part * scales[kind], axis=0, keepdims=True
            )
            normed = normed * gains[kind, number : number + 1]
            sums[kind] = sums[kind] + jnp.sum(part * normed, axis=1, keepdims=True)
            start = (kind * HEADS_HERE + number) * HEAD_DIM
            weighted[:, start : start + HEAD_DIM] = normed
    for kind in range(2):
        inner[0, kind : kind + 1] = to_row(sums[kind])


def input_grad_kernel(weighted, qkv, squares, inner, value_grad, weights, qkv_grad, out):
    for kind in range(2):
        scale = scale_of(squares[0], kind)
        shift_by = scale * scale * scale * (to_column(inner[0][kind : kind + 1]) / D)
        for number in range(HEADS_HERE):
            start = (kind * HEADS_HERE + number) * HEAD_DIM
            part = weighted[:, start : start + HEAD_DIM]
            start = (number * 3 + kind) * HEAD_DIM
            qkv_grad[:, start : start + HEAD_DIM] = (
                scale * part - head(qkv, kind, number) * shift_by
            ).astype(BF16)
    for number in range(HEADS_HERE):
        start = (number * 3 + 2) * HEAD_DIM
        qkv_grad[:, start : start + HEAD_DIM] = pair(value_grad, number)
    out[...] = mm(qkv_grad[...], weights[...], NT).astype(BF16)


class Place:
    def __init__(self, reps):
        self.reps = reps
        self.g = lax.axis_index("g")
        self.q = lax.axis_index("q")
        self.c = lax.axis_index("c")
        self.x = lax.axis_index("x")

    def orders(self):
        return [
            [
                (g * self.reps + (q ^ flip)) * CORES + c
                for q in range(self.reps)
                for c in range(CORES)
                for g in range(GROUP)
            ]
            for flip in ((0, 1) if self.reps == 2 else (0,))
        ]

    def shuffle(self, value, orders):
        if self.reps == 2:
            return reorder(value, self.q, orders)
        rows, size = value.shape[0], D // len(orders[0])
        blocks = value.reshape(rows, -1, size)
        return jnp.stack([blocks[:, i] for i in orders[0]], 1).reshape(rows, D)

    def to_local(self, value):
        return self.shuffle(value, self.orders())

    def to_global(self, value):
        return self.shuffle(
            value, [[order.index(i) for i in range(len(order))] for order in self.orders()]
        )

    def send(self, pieces):
        return [pieces[0]] + [shift(pieces[by], by) for by in range(1, GROUP)]

    def spread(self, shards):
        return self.send(pack(shards, self.g))

    def settle(self, pieces):
        mine, other = sort(pieces, self.g, self.c)
        return [mine, swap(other, "c")]

    def settled(self, halves):
        return by_core(*halves, self.c)

    def widen(self, held):
        if self.reps != 2:
            return [lax.all_gather(held, "q", axis=0, tiled=True)]
        return [held, swap(held, "q"), swap(held, "x")]

    def widened(self, blocks):
        if self.reps != 2:
            return [*blocks, swap(blocks[0], "x")]
        half = blocks[0].shape[0] // 2
        return [*blocks, swap(blocks[2][:half], "q"), swap(blocks[1][half:], "x")]

    def join(self, blocks, cuts):
        rows = blocks[0].shape[0]
        spots = [(0, 0), (0, 1)]
        if self.reps == 2:
            spots = [(0, 0), (rows, 0), (0, 1), (rows, 1), (rows + rows // 2, 1)]
        moves, shapes = [], [(D, 2 * (stop - start)) for start, stop in cuts]
        for number, (start, stop) in enumerate(cuts):
            for at, (row, side) in enumerate(spots):
                moves.append((at, (start, stop), number, row, side * (stop - start)))
        return assemble(blocks, moves, shapes)

    def narrow(self, parts):
        if self.reps != 2:
            return [swap(parts[1], "x")]
        return [swap(parts[0], "q"), swap(parts[1], "x")]

    def narrow_next(self, parts, came):
        if self.reps != 2:
            total = add(parts[0], came[0])
            return [lax.psum_scatter(total, "q", scatter_dimension=0, tiled=True)]
        _, _, beside_top, below_low, _ = parts
        return [swap(add(beside_top, came[0][0]), "x"), swap(add(below_low, came[1][0]), "q")]

    def narrowed(self, parts, came, more):
        if self.reps != 2:
            return jnp.split(more[0], 2)
        half = parts[4].shape[0] // 2
        return (
            add(parts[4][:half], more[0], came[0][1]),
            add(parts[4][half:], came[1][1], more[1]),
        )

    def unsettle(self, halves):
        top, low = halves
        mine, other = jnp.where(self.c == 0, top, low), jnp.where(self.c == 0, low, top)
        return [mine, swap(other, "c")]

    def collect(self, halves):
        return self.send(deal(*halves, self.g, self.c))


def rope_tables(segments):
    places = jnp.arange(segments.shape[1], dtype=jnp.int32)
    same = segments[:, :, None] == segments[:, None, :]
    earlier = same & (places[None, None, :] < places[None, :, None])
    spot = jnp.sum(earlier.astype(jnp.int32), axis=2).astype(F32)
    halfway = HEAD_DIM // 2
    inverse = jnp.exp(jnp.arange(halfway, dtype=F32) * (-2.0 * math.log(ROPE_BASE) / HEAD_DIM))
    angles = spot.reshape(-1, 1) * inverse
    cosine, sine = jnp.cos(angles), jnp.sin(angles)
    return jnp.concatenate([cosine, cosine], 1), jnp.concatenate([-sine, sine], 1)


def norm_scale(values):
    return lax.rsqrt(jnp.mean(values * values, axis=-1, keepdims=True) + EPSILON)


def norm_back(values, scale, gain, grad):
    weighted = grad * gain
    inner = jnp.sum(values * weighted, axis=-1, keepdims=True) / D
    return (
        scale * weighted - values * (scale * scale * scale) * inner,
        jnp.sum(grad * values * scale, axis=0),
    )


def on_device(
    reps,
    tokens,
    segment_ids,
    query_proj,
    key_proj,
    value_proj,
    out_proj,
    query_gain,
    key_gain,
    attn_gain,
    gate_proj,
    up_proj,
    down_proj,
    mlp_gain,
    cotangent,
):
    place = Place(reps)
    slots = GROUP * CORES
    shard_rows = query_proj.shape[0]
    length = tokens.shape[2]
    slot = place.g * CORES + place.c

    step = Order()
    count = slots * length
    cut = 3 * HEAD_DIM

    def team_scatter(value):
        return lax.psum_scatter(value, TEAM, scatter_dimension=0, tiled=True)

    def team_gather(value):
        return lax.all_gather(value, TEAM, axis=0, tiled=True)

    def team_sum(value):
        value = value + step(swap(value, "c"))
        for by in (1, 2):
            value = value + step(
                lax.ppermute(value, "g", [(i, i ^ by) for i in range(GROUP)])
            )
        return value

    attn = place.spread([query_proj, key_proj, value_proj, out_proj])
    own_row = place.to_local(pick(tokens, place.x, 0)[0])
    segments = pick(segment_ids, place.x, 0)
    segments = ordered(place.c, segments, swap(segments, "c"), 0)[:, 0]
    gate = pack([gate_proj, up_proj], place.g)
    feed = pack([down_proj], place.g)
    attn, own_row, segments, gate, feed = step(attn, own_row, segments, gate, feed)
    all_rows = team_gather(own_row)
    segments = [segments] + [shift(segments, by) for by in range(1, GROUP)]
    attn = step(place.settle(attn))
    attn = place.widen(place.settled(attn))
    gains = jnp.stack([pick(w.reshape(slots, HEAD_DIM), slot, 0) for w in (query_gain, key_gain)])
    gains = jnp.stack([gains, swap(gains, "x")], 1)
    gathered = jnp.zeros((GROUP,) + segments[0].shape, segments[0].dtype)
    for by, piece in enumerate(segments):
        gathered = put(gathered, piece, (place.g - by) % GROUP)
    segments = gathered.reshape(slots, length)
    cosine, sine = rope_tables(segments)
    segments = segments.astype(F32)[:, None]
    attn, gains, segments, gate = step(attn, gains, segments, gate)
    gate = place.send(gate)
    attn = step(place.widened(attn))
    qkv_full, out_full = step(place.join(attn, [(0, cut), (cut, 4 * HEAD_DIM)]))
    all_rows, cosine, sine = step(all_rows, cosine, sine)

    qkv, squares = step(
        *row_call(
            project_kernel,
            slots,
            [(all_rows, length), (qkv_full, "whole")],
            [((count, 6 * HEAD_DIM), F32, length), ((slots, 2, length), F32, 1)],
        )
    )
    gate = step(place.settle(step(gate)))
    gate = place.widen(place.settled(gate))
    squares = team_sum(squares)
    squares, feed = step(squares, feed)
    feed = place.send(feed)
    low = ((count, 2 * HEAD_DIM), BF16, length)
    query_low, key_low, value_low, mixed, attn_part = step(
        *row_call(
            attend_kernel,
            slots,
            [
                (qkv, length),
                (squares, 1),
                (gains, "whole"),
                (cosine, length),
                (sine, length),
                (segments, 1),
                (out_full, "whole"),
            ],
            [low, low, low, low, ((count, D), BF16, length)],
        )
    )
    attn_part, gate, feed = step(attn_part, gate, feed)
    projected = team_scatter(attn_part)
    gate = place.widened(gate)
    feed = place.settle(feed)
    feed = place.widen(place.settled(step(feed)))
    gate = step(gate)
    width = gate_proj.shape[1] // slots
    projected = step(projected)
    projected = projected.astype(F32)
    attn_gain, mlp_gain = place.to_local(jnp.stack([attn_gain, mlp_gain]))
    projected_scale = norm_scale(projected)
    hidden = own_row.astype(F32) + projected * projected_scale * attn_gain
    hidden_low, hidden = step(hidden.astype(BF16), hidden)
    hidden_all = team_gather(hidden_low)
    gate_full, up_full = step(place.join(gate, [(0, width), (width, 2 * width)]))
    feed = place.widened(step(feed))
    [down_full] = place.join(step(feed), [(0, width)])
    own_cotangent = place.to_local(pick(cotangent, place.x, 0)[0]).astype(F32)
    hidden_all, gate_full, up_full, down_full, own_cotangent = step(
        hidden_all, gate_full, up_full, down_full, own_cotangent
    )

    lifted = dot(hidden_all, up_full)
    gated = dot(hidden_all, gate_full)
    active = (gated / (1.0 + jnp.exp(-gated)) * lifted).astype(BF16)
    reduced = team_scatter(step(dot_nt(active, down_full).astype(BF16)))
    reduced = step(reduced).astype(F32)
    reduced_scale = norm_scale(reduced)
    reduced_grad, mlp_gain_grad = norm_back(reduced, reduced_scale, mlp_gain, own_cotangent)
    reduced_all = team_gather(step(reduced_grad.astype(BF16)))
    own_out = place.to_global((hidden + reduced * reduced_scale * mlp_gain).astype(BF16))
    layer_out = ordered(place.x, own_out, swap(own_out, "x"), 0)[:, None]
    reduced_all, mlp_gain_grad, layer_out = step(reduced_all, mlp_gain_grad, layer_out)

    active_grad = dot(reduced_all, down_full)
    gate_sigmoid = 1.0 / (1.0 + jnp.exp(-gated))
    gated_grad = (
        active_grad * lifted * gate_sigmoid * (1.0 + gated * (1.0 - gate_sigmoid))
    ).astype(BF16)
    lifted_grad = (active_grad * gated * gate_sigmoid).astype(BF16)
    hidden_part = dot_nt(gated_grad, gate_full) + dot_nt(lifted_grad, up_full)
    hidden_part, gated_grad, lifted_grad = step(hidden_part.astype(BF16), gated_grad, lifted_grad)
    hidden_part = team_scatter(hidden_part)
    down = step(weight_grads([(reduced_all, active)], reps, [width]))
    down_came = place.narrow(down)
    feed = step(
        weight_grads([(hidden_all, gated_grad), (hidden_all, lifted_grad)], reps, [width, width])
    )
    down_came = step(down_came)
    down_more = place.narrow_next(down, down_came)
    hidden_grad = own_cotangent + step(hidden_part).astype(F32)
    projected_grad, attn_gain_grad = norm_back(projected, projected_scale, attn_gain, hidden_grad)
    projected_low, hidden_grad, attn_gain_grad = step(
        projected_grad.astype(BF16), hidden_grad, attn_gain_grad
    )
    projected_all = team_gather(projected_low)
    down_more, feed = step(down_more, feed)
    feed_came = place.narrow(feed)
    down = step(place.unsettle(place.narrowed(down, down_came, down_more)))
    norm_gain_grads = place.to_global(jnp.stack([attn_gain_grad, mlp_gain_grad]))
    down = deal(*down, place.g, place.c)
    norm_gain_grads, down = step(norm_gain_grads, down)

    projected_all, down = step(projected_all, down)
    down = place.send(down)
    weighted, value_grad, inner, head_gain_grads = step(
        *row_call(
            attend_back_kernel,
            slots,
            [
                (projected_all, length),
                (out_full, "whole"),
                (query_low, length),
                (key_low, length),
                (value_low, length),
                (qkv, length),
                (squares, 1),
                (gains, "whole"),
                (cosine, length),
                (sine, length),
                (segments, 1),
            ],
            [
                ((count, 4 * HEAD_DIM), F32, length),
                low,
                ((slots, 2, length), F32, 1),
                (gains.shape, F32, "whole"),
            ],
        )
    )
    spots = jnp.zeros((2, 2, slots, HEAD_DIM), F32)
    for number in range(2):
        spots = lax.dynamic_update_slice(
            spots,
            head_gain_grads[:, number][:, None, None],
            (0, place.x if number == 0 else 1 - place.x, slot, 0),
        )
    message = jnp.concatenate([v.reshape(-1, HEAD_DIM) for v in (inner, spots, norm_gain_grads)])
    message, feed_came = step(message, feed_came)
    feed_more = place.narrow_next(feed, feed_came)
    down = step(down)
    message = team_sum(message)
    inner, gain_grads = message[: 2 * slots].reshape(inner.shape), message[2 * slots :]
    qkv_grad, input_part = step(
        *row_call(
            input_grad_kernel,
            slots,
            [
                (weighted, length),
                (qkv, length),
                (squares, 1),
                (inner, 1),
                (value_grad, length),
                (qkv_full, "whole"),
            ],
            [((count, 6 * HEAD_DIM), BF16, length), ((count, D), BF16, length)],
        )
    )
    input_part = team_scatter(input_part)
    feed = place.unsettle(place.narrowed(feed, feed_came, step(feed_more)))
    feed = place.collect(step(feed))
    attn = step(
        weight_grads([(all_rows, qkv_grad), (projected_all, mixed)], reps, [cut, HEAD_DIM])
    )
    attn_came = place.narrow(attn)
    [down_grad] = step(unpack(down, place.g, 1))
    attn_came = step(attn_came)
    attn_more = place.narrow_next(attn, attn_came)
    gain_x = swap(gain_grads, "x")
    feed = step(feed)
    attn_more = step(attn_more)
    attn = place.unsettle(place.narrowed(attn, attn_came, attn_more))
    attn, gain_x = step(attn, gain_x)
    attn = place.collect(attn)
    gain_grads = gain_grads + gain_x
    gain_q = swap(gain_grads, "q") if reps == 2 else lax.psum(gain_grads, "q") - gain_grads
    gate_grad, up_grad = step(unpack(feed, place.g, 2))
    input_part, gain_q = step(input_part, gain_q)
    own_grad = place.to_global((hidden_grad + input_part.astype(F32)).astype(BF16))
    own_grad_x = swap(own_grad, "x")
    summed = (gain_grads + gain_q).reshape(4, D)
    attn_grads = unpack(step(attn), place.g, 4)
    tokens_grad = ordered(place.x, own_grad, step(own_grad_x), 0)[:, None].astype(F32)
    summed = summed + step.token
    half_of = lambda v: pick(v.reshape(2, -1), place.x, 0)
    return (
        layer_out,
        tokens_grad,
        *attn_grads,
        half_of(summed[0]),
        half_of(summed[1]),
        summed[2],
        gate_grad,
        up_grad,
        down_grad,
        summed[3],
    )


def solution(mesh):
    reps = mesh.shape["dp"] // (GROUP * CORES)
    folded = Mesh(
        mesh.devices.reshape(GROUP, reps, CORES, mesh.shape["tensor"]), ("g", "q", "c", "x")
    )
    dp = ("g", "q", "c")
    row = P(None, dp, None, None)
    weight = P(dp, "x")
    gain = P("x")
    in_specs = (row, P(None, dp, None)) + (weight,) * 4 + (gain, gain, P()) + (weight,) * 3
    in_specs += (P(), row)
    out_specs = (row, row) + (weight,) * 4 + (gain, gain, P()) + (weight,) * 3 + (P(),)

    def body(*args):
        return on_device(reps, *args)

    return jax.shard_map(
        body, mesh=folded, in_specs=in_specs, out_specs=out_specs, check_vma=False
    )
```

```python
import math

import jax
import jax.numpy as jnp
from jax import lax
from jax.experimental import pallas as pl
from jax.experimental.pallas import tpu as pltpu
from jax.sharding import Mesh, PartitionSpec as P

D = 2048
HEAD_DIM = 128
EPSILON = 1e-06
ROPE_BASE = 500000.0
GROUP = 4
CORES = 2
F32 = jnp.float32
BF16 = jnp.bfloat16
TEAM = ("g", "c")


def dot(a, b):
    return jnp.dot(a, b, preferred_element_type=F32)


def dot_nt(a, b):
    return lax.dot_general(a, b, (((1,), (1,)), ((), ())), preferred_element_type=F32)


def dot_tn(a, b):
    return lax.dot_general(a, b, (((0,), (0,)), ((), ())), preferred_element_type=F32)


def swap(value, axis):
    return lax.ppermute(value, axis, [(0, 1), (1, 0)])


def shift(value, by):
    return lax.ppermute(value, "g", [(i, (i + by) % GROUP) for i in range(GROUP)])


def pick(value, index, axis):
    return lax.dynamic_index_in_dim(value, index, axis, keepdims=False)


def put(value, piece, index, axis=0):
    return lax.dynamic_update_index_in_dim(value, piece, index, axis)


def ordered(flag, first, second, axis):
    return jnp.where(
        flag == 0, jnp.stack([first, second], axis), jnp.stack([second, first], axis)
    )


def add(*values):
    return sum(v.astype(F32) for v in values).astype(BF16)


class Order:
    def __init__(self):
        self.token = jnp.zeros((), F32)

    def __call__(self, *values):
        *values, self.token = lax.optimization_barrier((*values, self.token))
        return values[0] if len(values) == 1 else values


def assemble(pieces, moves, shapes):
    def kernel(*refs):
        sources, (*targets, sems) = refs[: len(pieces)], refs[len(pieces) :]
        copies = []
        for number, (source, columns, target, row, column) in enumerate(moves):
            rows, width = pieces[source].shape[0], columns[1] - columns[0]
            copies.append(
                pltpu.make_async_copy(
                    sources[source].at[:, pl.ds(columns[0], width)],
                    targets[target].at[pl.ds(row, rows), pl.ds(column, width)],
                    sems.at[number],
                )
            )
        for copy in copies:
            copy.start()
        for copy in copies:
            copy.wait()

    out = pl.pallas_call(
        kernel,
        out_shape=[jax.ShapeDtypeStruct(shape, pieces[0].dtype) for shape in shapes],
        in_specs=[pl.BlockSpec(memory_space=pl.ANY)] * len(pieces),
        out_specs=[pl.BlockSpec(memory_space=pltpu.VMEM)] * len(shapes),
        scratch_shapes=[pltpu.SemaphoreType.DMA((len(moves),))],
        compiler_params=pltpu.CompilerParams(vmem_limit_bytes=24 << 20),
        cost_estimate=pl.CostEstimate(
            flops=0,
            bytes_accessed=sum(4 * math.prod(shape) for shape in shapes),
            transcendentals=0,
        ),
    )(*pieces)
    return out


def reorder(values, flag, orders):
    size = values.shape[1] // len(orders[0])

    def kernel(flag_ref, source, target):
        for number, order in enumerate(orders):

            @pl.when(flag_ref[0] == number)
            def _():
                for to, block in enumerate(order):
                    target[:, to * size : (to + 1) * size] = source[
                        :, block * size : (block + 1) * size
                    ]

    return pl.pallas_call(
        kernel,
        out_shape=jax.ShapeDtypeStruct(values.shape, values.dtype),
        in_specs=[
            pl.BlockSpec(memory_space=pltpu.SMEM),
            pl.BlockSpec(memory_space=pltpu.VMEM),
        ],
        out_specs=pl.BlockSpec(memory_space=pltpu.VMEM),
        cost_estimate=pl.CostEstimate(
            flops=0, bytes_accessed=4 * values.size, transcendentals=0
        ),
    )(jnp.reshape(flag, (1,)).astype(jnp.int32), values)


def vmem_call(kernel, shapes, scalars, arrays):
    flags = jnp.stack([jnp.asarray(v, jnp.int32) for v in scalars])
    spec = pl.BlockSpec(memory_space=pltpu.VMEM)
    return pl.pallas_call(
        kernel,
        out_shape=shapes,
        in_specs=[pl.BlockSpec(memory_space=pltpu.SMEM)] + [spec] * len(arrays),
        out_specs=[spec] * len(shapes),
        compiler_params=pltpu.CompilerParams(vmem_limit_bytes=VMEM_LIMIT),
        cost_estimate=pl.CostEstimate(flops=0, bytes_accessed=LOCAL_BYTES, transcendentals=0),
    )(flags, *arrays)


def pack(shards, g):
    rows, width = shards[0].shape[0], shards[0].shape[1] // (GROUP * CORES)
    count = len(shards)

    def kernel(flags, *refs):
        sources, targets = refs[:count], refs[count:]
        for by in range(GROUP):
            to = lax.rem(flags[0] + by, GROUP)
            for core in range(CORES):
                start = pl.multiple_of((to * CORES + core) * width, width)
                for number in range(count):
                    at = (core * count + number) * width
                    targets[by][:, at : at + width] = sources[number][:, pl.ds(start, width)]

    shape = jax.ShapeDtypeStruct((rows, CORES * count * width), shards[0].dtype)
    return vmem_call(kernel, [shape] * GROUP, [g], shards)


def sort(pieces, g, c):
    rows, half = pieces[0].shape[0], pieces[0].shape[1] // CORES

    def kernel(flags, *refs):
        sources, targets = refs[:GROUP], refs[GROUP:]
        for by in range(GROUP):
            row = pl.multiple_of(lax.rem(flags[0] + GROUP - by, GROUP) * rows, rows)
            for number in range(CORES):
                core = flags[1] if number == 0 else 1 - flags[1]
                targets[number][pl.ds(row, rows), :] = sources[by][
                    :, pl.ds(pl.multiple_of(core * half, half), half)
                ]

    shape = jax.ShapeDtypeStruct((GROUP * rows, half), pieces[0].dtype)
    return vmem_call(kernel, [shape] * CORES, [g, c], pieces)


def unpack(pieces, g, count):
    rows, width = pieces[0].shape[0], pieces[0].shape[1] // (CORES * count)

    def kernel(flags, *refs):
        sources, targets = refs[:GROUP], refs[GROUP:]
        for by in range(GROUP):
            source = lax.rem(flags[0] + GROUP - by, GROUP)
            for core in range(CORES):
                start = pl.multiple_of((source * CORES + core) * width, width)
                for number in range(count):
                    at = (core * count + number) * width
                    targets[number][:, pl.ds(start, width)] = sources[by][
                        :, at : at + width
                    ].astype(F32)

    shape = jax.ShapeDtypeStruct((rows, GROUP * CORES * width), F32)
    return vmem_call(kernel, [shape] * count, [g], pieces)


def by_core(mine, got, c):
    rows = mine.shape[0]

    def kernel(flags, first, second, target):
        target[pl.ds(pl.multiple_of(flags[0] * rows, rows), rows), :] = first[...]
        target[pl.ds(pl.multiple_of((1 - flags[0]) * rows, rows), rows), :] = second[...]

    [out] = vmem_call(
        kernel,
        [jax.ShapeDtypeStruct((CORES * rows, mine.shape[1]), mine.dtype)],
        [c],
        [mine, got],
    )
    return out


def deal(mine, got, g, c):
    rows, width = mine.shape[0] // GROUP, mine.shape[1]

    def kernel(flags, first, second, *targets):
        for by in range(GROUP):
            row = pl.multiple_of(lax.rem(flags[0] + by, GROUP) * rows, rows)
            for number, source in enumerate((first, second)):
                core = flags[1] if number == 0 else 1 - flags[1]
                at = pl.ds(pl.multiple_of(core * width, width), width)
                targets[by][:, at] = source[pl.ds(row, rows), :]

    shape = jax.ShapeDtypeStruct((rows, CORES * width), mine.dtype)
    return vmem_call(kernel, [shape] * GROUP, [g, c], [mine, got])


def weight_grads(factors, reps, cuts):
    step = 256
    count = factors[0][0].shape[0]
    total = sum(cuts)
    starts = [sum(cuts[:number]) for number in range(len(cuts))]

    def products(lefts, rights, own, other):
        for left, right, start, width in zip(lefts, rights, starts, cuts):
            product = mm(left[...], right[...], TN).astype(BF16)
            own[:, start : start + width] = product[:, :width]
            other[:, start : start + width] = product[:, width:]

    lefts = [left for left, _ in factors]
    rights = [right for _, right in factors]
    size = len(factors)
    whole = [pl.BlockSpec(v.shape, lambda i: (0, 0)) for v in rights]
    params = {
        "compiler_params": pltpu.CompilerParams(vmem_limit_bytes=VMEM_LIMIT),
        "cost_estimate": pl.CostEstimate(flops=0, bytes_accessed=LOCAL_BYTES, transcendentals=0),
    }
    if reps != 2:

        def kernel(*refs):
            products(refs[:size], refs[size : 2 * size], *refs[2 * size :])

        out = pl.BlockSpec((step, total), lambda i: (i, 0))
        return pl.pallas_call(
            kernel,
            grid=(D // step,),
            in_specs=[pl.BlockSpec((count, step), lambda i: (0, i))] * size + whole,
            out_specs=[out, out],
            out_shape=[jax.ShapeDtypeStruct((D, total), BF16)] * 2,
            **params,
        )(*lefts, *rights)

    steps = D // 2 // step
    half = steps // 2

    def kernel(*refs):
        upper, lower, right = refs[:size], refs[size : 2 * size], refs[2 * size : 3 * size]
        to_q, to_x, beside_top, below_low, keep = refs[3 * size :]

        @pl.when(pl.program_id(0) < half)
        def _():
            products(upper, right, keep, beside_top)
            products(lower, right, to_q.at[1], to_q.at[0])

        @pl.when(pl.program_id(0) >= half)
        def _():
            products(upper, right, keep, to_x.at[1])
            products(lower, right, below_low, to_x.at[0])

    first = lambda i: jnp.minimum(i, half - 1)
    last = lambda i: jnp.maximum(i - half, 0)
    rows = D // 4
    return pl.pallas_call(
        kernel,
        grid=(steps,),
        in_specs=[pl.BlockSpec((count, step), lambda i: (0, i))] * size
        + [pl.BlockSpec((count, step), lambda i: (0, i + steps))] * size
        + whole,
        out_specs=[
            pl.BlockSpec((2, step, total), lambda i: (0, first(i), 0)),
            pl.BlockSpec((2, step, total), lambda i: (0, last(i), 0)),
            pl.BlockSpec((step, total), lambda i: (first(i), 0)),
            pl.BlockSpec((step, total), lambda i: (last(i), 0)),
            pl.BlockSpec((step, total), lambda i: (i, 0)),
        ],
        out_shape=[
            jax.ShapeDtypeStruct(shape, BF16)
            for shape in (
                (2, rows, total), (2, rows, total), (rows, total), (rows, total), (2 * rows, total)
            )
        ],
        **params,
    )(*lefts, *lefts, *rights)


NN, NT, TN = ((1,), (0,)), ((1,), (1,)), ((0,), (0,))
VMEM_LIMIT = 60 << 20
LOCAL_BYTES = 200 << 20
HEADS_HERE = 2
ROWS = 2
LENGTH = 128
ROOT = HEAD_DIM ** (-0.5)


def mm(a, b, dims=NN):
    return lax.dot_general(a, b, (dims, ((), ())), preferred_element_type=F32)


def eye(size):
    return lax.broadcasted_iota(jnp.int32, (size, size), 0) == lax.broadcasted_iota(
        jnp.int32, (size, size), 1
    )


def to_column(row):
    return jnp.sum(jnp.where(eye(row.shape[1]), row, 0.0), axis=1, keepdims=True)


def to_row(column):
    return jnp.sum(jnp.where(eye(column.shape[0]), column, 0.0), axis=0, keepdims=True)


def head(values, kind, number):
    start = (number * 3 + kind) * HEAD_DIM
    return values[:, start : start + HEAD_DIM]


def pair(values, number):
    return values[:, number * HEAD_DIM : (number + 1) * HEAD_DIM]


def rotated(values, cosine, sine):
    return values * cosine + pltpu.roll(values, HEAD_DIM // 2, 1) * sine


def allowed_keys(segment_row):
    size = segment_row.shape[1]
    same = to_column(segment_row) == segment_row
    later = lax.broadcasted_iota(jnp.int32, (size, size), 1) > lax.broadcasted_iota(
        jnp.int32, (size, size), 0
    )
    return jnp.logical_and(same, jnp.logical_not(later))


def softmax_of(query, key, allowed):
    scores = jnp.where(allowed, mm(query, key, NT) * ROOT, -1e30)
    expo = jnp.exp(scores - jnp.max(scores, axis=1, keepdims=True))
    return expo / jnp.sum(expo, axis=1, keepdims=True)


def scale_of(squares, kind):
    return to_column(lax.rsqrt(squares[kind : kind + 1] / D + EPSILON))


def row_call(kernel, rows, ins, outs):
    def spec(shape, block):
        if block == "whole":
            return pl.BlockSpec(shape, lambda i: (0,) * len(shape))
        return pl.BlockSpec((ROWS * block,) + shape[1:], lambda i: (i,) + (0,) * (len(shape) - 1))

    return pl.pallas_call(
        kernel,
        grid=(rows // ROWS,),
        in_specs=[spec(v.shape, block) for v, block in ins],
        out_specs=[spec(shape, block) for shape, _, block in outs],
        out_shape=[jax.ShapeDtypeStruct(shape, dtype) for shape, dtype, _ in outs],
        compiler_params=pltpu.CompilerParams(vmem_limit_bytes=VMEM_LIMIT),
        cost_estimate=pl.CostEstimate(flops=0, bytes_accessed=0, transcendentals=0),
    )(*[v for v, _ in ins])


def row_views(row, *refs):
    return [ref.at[row * LENGTH : (row + 1) * LENGTH] for ref in refs]


def project_kernel(tokens, weights, out, squares):
    out[...] = mm(tokens[...], weights[...])
    for row in range(ROWS):
        [product] = row_views(row, out)
        for kind in range(2):
            total = 0.0
            for number in range(HEADS_HERE):
                part = head(product, kind, number)
                total = total + jnp.sum(part * part, axis=1, keepdims=True)
            squares[row, kind : kind + 1] = to_row(total)


def attend_kernel(
    qkv_all, squares, gains, cosine_all, sine_all, segments, weights,
    query_all, key_all, value_all, mixed_all, out,
):
    for row in range(ROWS):
        qkv, cosine, sine, query_out, key_out, value_out, mixed = row_views(
            row, qkv_all, cosine_all, sine_all, query_all, key_all, value_all, mixed_all
        )
        allowed = allowed_keys(segments[row])
        scales = [scale_of(squares[row], kind) for kind in range(2)]
        for number in range(HEADS_HERE):
            low = [
                rotated(
                    head(qkv, kind, number) * scales[kind] * gains[kind, number : number + 1],
                    cosine[...],
                    sine[...],
                ).astype(BF16)
                for kind in range(2)
            ]
            value = head(qkv, 2, number).astype(BF16)
            probs = softmax_of(*low, allowed).astype(BF16)
            where = slice(number * HEAD_DIM, (number + 1) * HEAD_DIM)
            query_out[:, where] = low[0]
            key_out[:, where] = low[1]
            value_out[:, where] = value
            mixed[:, where] = mm(probs, value).astype(BF16)
    out[...] = mm(mixed_all[...], weights[...], NT).astype(BF16)


def attend_back_kernel(
    grads, weights, query_all, key_all, value_all, qkv_all, squares, gains, cosine_all, sine_all,
    segments, weighted_all, value_grad_all, inner, gain_grad,
):
    @pl.when(pl.program_id(0) == 0)
    def _():
        gain_grad[...] = jnp.zeros_like(gain_grad)

    mixed_grads = mm(grads[...], weights[...]).astype(BF16)
    for row in range(ROWS):
        queries, keys, values, qkv, cosine, sine, weighted, value_grad = row_views(
            row, query_all, key_all, value_all, qkv_all, cosine_all, sine_all, weighted_all,
            value_grad_all,
        )
        allowed = allowed_keys(segments[row])
        scales = [scale_of(squares[row], kind) for kind in range(2)]
        sums = [0.0, 0.0]
        for number in range(HEADS_HERE):
            query, key, value = pair(queries, number), pair(keys, number), pair(values, number)
            mixed_grad = pair(mixed_grads[row * LENGTH : (row + 1) * LENGTH], number)
            probs = softmax_of(query, key, allowed)
            where = slice(number * HEAD_DIM, (number + 1) * HEAD_DIM)
            value_grad[:, where] = mm(probs.astype(BF16), mixed_grad, TN).astype(BF16)
            prob_grad = mm(mixed_grad, value, NT)
            score_grad = probs * (prob_grad - jnp.sum(probs * prob_grad, axis=1, keepdims=True))
            score_low = (score_grad * ROOT).astype(BF16)
            turned = (mm(score_low, key), mm(score_low, query, TN))
            for kind in range(2):
                normed = rotated(turned[kind], cosine[...], -sine[...])
                part = head(qkv, kind, number)
                gain_grad[kind, number : number + 1] += jnp.sum(
                    normed * part * scales[kind], axis=0, keepdims=True
                )
                normed = normed * gains[kind, number : number + 1]
                sums[kind] = sums[kind] + jnp.sum(part * normed, axis=1, keepdims=True)
                start = (kind * HEADS_HERE + number) * HEAD_DIM
                weighted[:, start : start + HEAD_DIM] = normed
        for kind in range(2):
            inner[row, kind : kind + 1] = to_row(sums[kind])


def input_grad_kernel(
    weighted_all, qkv_all, squares, inner, value_grad_all, weights, qkv_grad_all, out
):
    for row in range(ROWS):
        weighted, qkv, value_grad, qkv_grad = row_views(
            row, weighted_all, qkv_all, value_grad_all, qkv_grad_all
        )
        for kind in range(2):
            scale = scale_of(squares[row], kind)
            shift_by = scale * scale * scale * (to_column(inner[row][kind : kind + 1]) / D)
            for number in range(HEADS_HERE):
                start = (kind * HEADS_HERE + number) * HEAD_DIM
                part = weighted[:, start : start + HEAD_DIM]
                start = (number * 3 + kind) * HEAD_DIM
                qkv_grad[:, start : start + HEAD_DIM] = (
                    scale * part - head(qkv, kind, number) * shift_by
                ).astype(BF16)
        for number in range(HEADS_HERE):
            start = (number * 3 + 2) * HEAD_DIM
            qkv_grad[:, start : start + HEAD_DIM] = pair(value_grad, number)
    out[...] = mm(qkv_grad_all[...], weights[...], NT).astype(BF16)


class Place:
    def __init__(self, reps):
        self.reps = reps
        self.g = lax.axis_index("g")
        self.q = lax.axis_index("q")
        self.c = lax.axis_index("c")
        self.x = lax.axis_index("x")

    def orders(self):
        return [
            [
                (g * self.reps + (q ^ flip)) * CORES + c
                for q in range(self.reps)
                for c in range(CORES)
                for g in range(GROUP)
            ]
            for flip in ((0, 1) if self.reps == 2 else (0,))
        ]

    def shuffle(self, value, orders):
        if self.reps == 2:
            return reorder(value, self.q, orders)
        rows, size = value.shape[0], D // len(orders[0])
        blocks = value.reshape(rows, -1, size)
        return jnp.stack([blocks[:, i] for i in orders[0]], 1).reshape(rows, D)

    def to_local(self, value):
        return self.shuffle(value, self.orders())

    def to_global(self, value):
        return self.shuffle(
            value, [[order.index(i) for i in range(len(order))] for order in self.orders()]
        )

    def send(self, pieces):
        return [pieces[0]] + [shift(pieces[by], by) for by in range(1, GROUP)]

    def spread(self, shards):
        return self.send(pack(shards, self.g))

    def settle(self, pieces):
        mine, other = sort(pieces, self.g, self.c)
        return [mine, swap(other, "c")]

    def settled(self, halves):
        return by_core(*halves, self.c)

    def widen(self, held):
        if self.reps != 2:
            return [lax.all_gather(held, "q", axis=0, tiled=True)]
        return [held, swap(held, "q"), swap(held, "x")]

    def widened(self, blocks):
        if self.reps != 2:
            return [*blocks, swap(blocks[0], "x")]
        half = blocks[0].shape[0] // 2
        return [*blocks, swap(blocks[2][:half], "q"), swap(blocks[1][half:], "x")]

    def join(self, blocks, cuts):
        rows = blocks[0].shape[0]
        spots = [(0, 0), (0, 1)]
        if self.reps == 2:
            spots = [(0, 0), (rows, 0), (0, 1), (rows, 1), (rows + rows // 2, 1)]
        moves, shapes = [], [(D, 2 * (stop - start)) for start, stop in cuts]
        for number, (start, stop) in enumerate(cuts):
            for at, (row, side) in enumerate(spots):
                moves.append((at, (start, stop), number, row, side * (stop - start)))
        return assemble(blocks, moves, shapes)

    def narrow(self, parts):
        if self.reps != 2:
            return [swap(parts[1], "x")]
        return [swap(parts[0], "q"), swap(parts[1], "x")]

    def narrow_next(self, parts, came):
        if self.reps != 2:
            total = add(parts[0], came[0])
            return [lax.psum_scatter(total, "q", scatter_dimension=0, tiled=True)]
        _, _, beside_top, below_low, _ = parts
        return [swap(add(beside_top, came[0][0]), "x"), swap(add(below_low, came[1][0]), "q")]

    def narrowed(self, parts, came, more):
        if self.reps != 2:
            return jnp.split(more[0], 2)
        half = parts[4].shape[0] // 2
        return (
            add(parts[4][:half], more[0], came[0][1]),
            add(parts[4][half:], came[1][1], more[1]),
        )

    def unsettle(self, halves):
        top, low = halves
        mine, other = jnp.where(self.c == 0, top, low), jnp.where(self.c == 0, low, top)
        return [mine, swap(other, "c")]

    def collect(self, halves):
        return self.send(deal(*halves, self.g, self.c))


def rope_tables(segments):
    places = jnp.arange(segments.shape[1], dtype=jnp.int32)
    same = segments[:, :, None] == segments[:, None, :]
    earlier = same & (places[None, None, :] < places[None, :, None])
    spot = jnp.sum(earlier.astype(jnp.int32), axis=2).astype(F32)
    halfway = HEAD_DIM // 2
    inverse = jnp.exp(jnp.arange(halfway, dtype=F32) * (-2.0 * math.log(ROPE_BASE) / HEAD_DIM))
    angles = spot.reshape(-1, 1) * inverse
    cosine, sine = jnp.cos(angles), jnp.sin(angles)
    return jnp.concatenate([cosine, cosine], 1), jnp.concatenate([-sine, sine], 1)


def norm_scale(values):
    return lax.rsqrt(jnp.mean(values * values, axis=-1, keepdims=True) + EPSILON)


def norm_back(values, scale, gain, grad):
    weighted = grad * gain
    inner = jnp.sum(values * weighted, axis=-1, keepdims=True) / D
    return (
        scale * weighted - values * (scale * scale * scale) * inner,
        jnp.sum(grad * values * scale, axis=0),
    )


def on_device(
    reps,
    tokens,
    segment_ids,
    query_proj,
    key_proj,
    value_proj,
    out_proj,
    query_gain,
    key_gain,
    attn_gain,
    gate_proj,
    up_proj,
    down_proj,
    mlp_gain,
    cotangent,
):
    place = Place(reps)
    slots = GROUP * CORES
    shard_rows = query_proj.shape[0]
    length = tokens.shape[2]
    slot = place.g * CORES + place.c

    step = Order()
    count = slots * length
    cut = 3 * HEAD_DIM

    def team_scatter(value):
        return lax.psum_scatter(value, TEAM, scatter_dimension=0, tiled=True)

    def team_gather(value):
        return lax.all_gather(value, TEAM, axis=0, tiled=True)

    def team_sum(value):
        value = value + step(swap(value, "c"))
        for by in (1, 2):
            value = value + step(
                lax.ppermute(value, "g", [(i, i ^ by) for i in range(GROUP)])
            )
        return value

    attn = place.spread([query_proj, key_proj, value_proj, out_proj])
    own_row = place.to_local(pick(tokens, place.x, 0)[0])
    segments = pick(segment_ids, place.x, 0)
    segments = ordered(place.c, segments, swap(segments, "c"), 0)[:, 0]
    gate = pack([gate_proj], place.g)
    feed = pack([up_proj, down_proj], place.g)
    attn, own_row, segments, gate, feed = step(attn, own_row, segments, gate, feed)
    all_rows = team_gather(own_row)
    segments = [segments] + [shift(segments, by) for by in range(1, GROUP)]
    attn = step(place.settle(attn))
    attn = place.widen(place.settled(attn))
    gains = jnp.stack([pick(w.reshape(slots, HEAD_DIM), slot, 0) for w in (query_gain, key_gain)])
    gains = jnp.stack([gains, swap(gains, "x")], 1)
    gathered = jnp.zeros((GROUP,) + segments[0].shape, segments[0].dtype)
    for by, piece in enumerate(segments):
        gathered = put(gathered, piece, (place.g - by) % GROUP)
    segments = gathered.reshape(slots, length)
    cosine, sine = rope_tables(segments)
    segments = segments.astype(F32)[:, None]
    attn, gains, segments, gate = step(attn, gains, segments, gate)
    gate = place.send(gate)
    attn = step(place.widened(attn))
    qkv_full, out_full = step(place.join(attn, [(0, cut), (cut, 4 * HEAD_DIM)]))
    all_rows, cosine, sine = step(all_rows, cosine, sine)

    qkv, squares = step(
        *row_call(
            project_kernel,
            slots,
            [(all_rows, length), (qkv_full, "whole")],
            [((count, 6 * HEAD_DIM), F32, length), ((slots, 2, length), F32, 1)],
        )
    )
    gate = step(place.settle(step(gate)))
    gate = place.widen(place.settled(gate))
    squares = team_sum(squares)
    squares, feed = step(squares, feed)
    feed = place.send(feed)
    low = ((count, 2 * HEAD_DIM), BF16, length)
    query_low, key_low, value_low, mixed, attn_part, gate = step(
        *row_call(
            attend_kernel,
            slots,
            [
                (qkv, length),
                (squares, 1),
                (gains, "whole"),
                (cosine, length),
                (sine, length),
                (segments, 1),
                (out_full, "whole"),
            ],
            [low, low, low, low, ((count, D), BF16, length)],
        ),
        gate,
    )
    gate = place.widened(gate)
    attn_part, gate, feed = step(attn_part, gate, feed)
    projected = team_scatter(attn_part)
    feed = place.settle(feed)
    feed = place.widen(place.settled(step(feed)))
    width = gate_proj.shape[1] // slots
    feed = step(feed)
    projected = step(projected)
    projected = projected.astype(F32)
    attn_gain, mlp_gain = place.to_local(jnp.stack([attn_gain, mlp_gain]))
    projected_scale = norm_scale(projected)
    hidden = own_row.astype(F32) + projected * projected_scale * attn_gain
    hidden_low, hidden = step(hidden.astype(BF16), hidden)
    hidden_all = team_gather(hidden_low)
    [gate_full] = step(place.join(gate, [(0, width)]))
    feed = place.widened(feed)
    up_full, down_full = place.join(step(feed), [(0, width), (width, 2 * width)])
    own_cotangent = place.to_local(pick(cotangent, place.x, 0)[0]).astype(F32)
    hidden_all, gate_full, up_full, down_full, own_cotangent = step(
        hidden_all, gate_full, up_full, down_full, own_cotangent
    )

    lifted = dot(hidden_all, up_full)
    gated = dot(hidden_all, gate_full)
    active = (gated / (1.0 + jnp.exp(-gated)) * lifted).astype(BF16)
    reduced = team_scatter(step(dot_nt(active, down_full).astype(BF16)))
    reduced = step(reduced).astype(F32)
    reduced_scale = norm_scale(reduced)
    reduced_grad, mlp_gain_grad = norm_back(reduced, reduced_scale, mlp_gain, own_cotangent)
    reduced_all = team_gather(step(reduced_grad.astype(BF16)))
    own_out = place.to_global((hidden + reduced * reduced_scale * mlp_gain).astype(BF16))
    layer_out = ordered(place.x, own_out, swap(own_out, "x"), 0)[:, None]
    reduced_all, mlp_gain_grad, layer_out = step(reduced_all, mlp_gain_grad, layer_out)

    active_grad = dot(reduced_all, down_full)
    gate_sigmoid = 1.0 / (1.0 + jnp.exp(-gated))
    gated_grad = (
        active_grad * lifted * gate_sigmoid * (1.0 + gated * (1.0 - gate_sigmoid))
    ).astype(BF16)
    lifted_grad = (active_grad * gated * gate_sigmoid).astype(BF16)
    hidden_part = dot_nt(gated_grad, gate_full) + dot_nt(lifted_grad, up_full)
    hidden_part, gated_grad, lifted_grad = step(hidden_part.astype(BF16), gated_grad, lifted_grad)
    hidden_part = team_scatter(hidden_part)
    down = step(weight_grads([(reduced_all, active)], reps, [width]))
    down_came = place.narrow(down)
    feed = step(
        weight_grads([(hidden_all, gated_grad), (hidden_all, lifted_grad)], reps, [width, width])
    )
    down_came = step(down_came)
    down_more = place.narrow_next(down, down_came)
    hidden_grad = own_cotangent + step(hidden_part).astype(F32)
    projected_grad, attn_gain_grad = norm_back(projected, projected_scale, attn_gain, hidden_grad)
    projected_low, hidden_grad, attn_gain_grad = step(
        projected_grad.astype(BF16), hidden_grad, attn_gain_grad
    )
    projected_all = team_gather(projected_low)
    down_more, feed = step(down_more, feed)
    feed_came = place.narrow(feed)
    down = step(place.unsettle(place.narrowed(down, down_came, down_more)))
    norm_gain_grads = place.to_global(jnp.stack([attn_gain_grad, mlp_gain_grad]))
    down = deal(*down, place.g, place.c)
    norm_gain_grads, down = step(norm_gain_grads, down)

    projected_all, down = step(projected_all, down)
    down = place.send(down)
    weighted, value_grad, inner, head_gain_grads, down, feed_came = step(
        *row_call(
            attend_back_kernel,
            slots,
            [
                (projected_all, length),
                (out_full, "whole"),
                (query_low, length),
                (key_low, length),
                (value_low, length),
                (qkv, length),
                (squares, 1),
                (gains, "whole"),
                (cosine, length),
                (sine, length),
                (segments, 1),
            ],
            [
                ((count, 4 * HEAD_DIM), F32, length),
                low,
                ((slots, 2, length), F32, 1),
                (gains.shape, F32, "whole"),
            ],
        ),
        down,
        feed_came,
    )
    spots = jnp.zeros((2, 2, slots, HEAD_DIM), F32)
    for number in range(2):
        spots = lax.dynamic_update_slice(
            spots,
            head_gain_grads[:, number][:, None, None],
            (0, place.x if number == 0 else 1 - place.x, slot, 0),
        )
    message = jnp.concatenate([v.reshape(-1, HEAD_DIM) for v in (inner, spots, norm_gain_grads)])
    feed_more = place.narrow_next(feed, feed_came)
    message = team_sum(message)
    inner, gain_grads = message[: 2 * slots].reshape(inner.shape), message[2 * slots :]
    gain_x = swap(gain_grads, "x")
    qkv_grad, input_part, feed_more, gain_x = step(
        *row_call(
            input_grad_kernel,
            slots,
            [
                (weighted, length),
                (qkv, length),
                (squares, 1),
                (inner, 1),
                (value_grad, length),
                (qkv_full, "whole"),
            ],
            [((count, 6 * HEAD_DIM), BF16, length), ((count, D), BF16, length)],
        ),
        feed_more,
        gain_x,
    )
    input_part = team_scatter(input_part)
    attn = step(
        weight_grads([(all_rows, qkv_grad), (projected_all, mixed)], reps, [cut, HEAD_DIM])
    )
    attn_came = place.narrow(attn)
    feed = step(place.unsettle(place.narrowed(feed, feed_came, feed_more)))
    feed = place.send(step(deal(*feed, place.g, place.c)))
    gain_grads = gain_grads + gain_x
    gain_q = swap(gain_grads, "q") if reps == 2 else lax.psum(gain_grads, "q") - gain_grads
    [down_grad] = step(unpack(down, place.g, 1))
    attn_came = step(attn_came)
    attn_more = place.narrow_next(attn, attn_came)
    feed = step(feed)
    attn_more = step(attn_more)
    attn = step(place.unsettle(place.narrowed(attn, attn_came, attn_more)))
    attn = place.send(step(deal(*attn, place.g, place.c)))
    input_part, gain_q = step(input_part, gain_q)
    summed = (gain_grads + gain_q).reshape(4, D)
    own_grad = place.to_global((hidden_grad + input_part.astype(F32)).astype(BF16))
    own_grad_x = swap(own_grad, "x")
    gate_grad, up_grad = unpack(feed, place.g, 2)
    attn_grads = unpack(step(attn), place.g, 4)
    tokens_grad = ordered(place.x, own_grad, step(own_grad_x), 0)[:, None].astype(F32)
    summed = summed + step.token
    half_of = lambda v: pick(v.reshape(2, -1), place.x, 0)
    return (
        layer_out,
        tokens_grad,
        *attn_grads,
        half_of(summed[0]),
        half_of(summed[1]),
        summed[2],
        gate_grad,
        up_grad,
        down_grad,
        summed[3],
    )


def solution(mesh):
    reps = mesh.shape["dp"] // (GROUP * CORES)
    folded = Mesh(
        mesh.devices.reshape(GROUP, reps, CORES, mesh.shape["tensor"]), ("g", "q", "c", "x")
    )
    dp = ("g", "q", "c")
    row = P(None, dp, None, None)
    weight = P(dp, "x")
    gain = P("x")
    in_specs = (row, P(None, dp, None)) + (weight,) * 4 + (gain, gain, P()) + (weight,) * 3
    in_specs += (P(), row)
    out_specs = (row, row) + (weight,) * 4 + (gain, gain, P()) + (weight,) * 3 + (P(),)

    def body(*args):
        return on_device(reps, *args)

    return jax.shard_map(
        body, mesh=folded, in_specs=in_specs, out_specs=out_specs, check_vma=False
    )
```

```python
import math

import jax
import jax.numpy as jnp
from jax import lax
from jax.experimental import pallas as pl
from jax.experimental.pallas import tpu as pltpu
from jax.sharding import Mesh, PartitionSpec as P

D = 2048
HEAD_DIM = 128
EPSILON = 1e-06
ROPE_BASE = 500000.0
GROUP = 4
CORES = 2
F32 = jnp.float32
BF16 = jnp.bfloat16
TEAM = ("g", "c")


def dot(a, b):
    return jnp.dot(a, b, preferred_element_type=F32)


def dot_nt(a, b):
    return lax.dot_general(a, b, (((1,), (1,)), ((), ())), preferred_element_type=F32)


def dot_tn(a, b):
    return lax.dot_general(a, b, (((0,), (0,)), ((), ())), preferred_element_type=F32)


def swap(value, axis):
    return lax.ppermute(value, axis, [(0, 1), (1, 0)])


def shift(value, by):
    return lax.ppermute(value, "g", [(i, (i + by) % GROUP) for i in range(GROUP)])


def pick(value, index, axis):
    return lax.dynamic_index_in_dim(value, index, axis, keepdims=False)


def put(value, piece, index, axis=0):
    return lax.dynamic_update_index_in_dim(value, piece, index, axis)


def ordered(flag, first, second, axis):
    return jnp.where(
        flag == 0, jnp.stack([first, second], axis), jnp.stack([second, first], axis)
    )


def add(*values):
    return sum(v.astype(F32) for v in values).astype(BF16)


class Order:
    def __init__(self):
        self.token = jnp.zeros((), F32)

    def __call__(self, *values):
        *values, self.token = lax.optimization_barrier((*values, self.token))
        return values[0] if len(values) == 1 else values


def assemble(pieces, moves, shapes):
    def kernel(*refs):
        sources, (*targets, sems) = refs[: len(pieces)], refs[len(pieces) :]
        copies = []
        for number, (source, columns, target, row, column) in enumerate(moves):
            rows, width = pieces[source].shape[0], columns[1] - columns[0]
            copies.append(
                pltpu.make_async_copy(
                    sources[source].at[:, pl.ds(columns[0], width)],
                    targets[target].at[pl.ds(row, rows), pl.ds(column, width)],
                    sems.at[number],
                )
            )
        for copy in copies:
            copy.start()
        for copy in copies:
            copy.wait()

    out = pl.pallas_call(
        kernel,
        out_shape=[jax.ShapeDtypeStruct(shape, pieces[0].dtype) for shape in shapes],
        in_specs=[pl.BlockSpec(memory_space=pl.ANY)] * len(pieces),
        out_specs=[pl.BlockSpec(memory_space=pltpu.VMEM)] * len(shapes),
        scratch_shapes=[pltpu.SemaphoreType.DMA((len(moves),))],
        compiler_params=pltpu.CompilerParams(vmem_limit_bytes=24 << 20),
        cost_estimate=pl.CostEstimate(
            flops=0,
            bytes_accessed=sum(4 * math.prod(shape) for shape in shapes),
            transcendentals=0,
        ),
    )(*pieces)
    return out


def reorder(values, flag, orders):
    size = values.shape[1] // len(orders[0])

    def kernel(flag_ref, source, target):
        for number, order in enumerate(orders):

            @pl.when(flag_ref[0] == number)
            def _():
                for to, block in enumerate(order):
                    target[:, to * size : (to + 1) * size] = source[
                        :, block * size : (block + 1) * size
                    ]

    return pl.pallas_call(
        kernel,
        out_shape=jax.ShapeDtypeStruct(values.shape, values.dtype),
        in_specs=[
            pl.BlockSpec(memory_space=pltpu.SMEM),
            pl.BlockSpec(memory_space=pltpu.VMEM),
        ],
        out_specs=pl.BlockSpec(memory_space=pltpu.VMEM),
        cost_estimate=pl.CostEstimate(
            flops=0, bytes_accessed=4 * values.size, transcendentals=0
        ),
    )(jnp.reshape(flag, (1,)).astype(jnp.int32), values)


def vmem_call(kernel, shapes, scalars, arrays):
    flags = jnp.stack([jnp.asarray(v, jnp.int32) for v in scalars])
    spec = pl.BlockSpec(memory_space=pltpu.VMEM)
    return pl.pallas_call(
        kernel,
        out_shape=shapes,
        in_specs=[pl.BlockSpec(memory_space=pltpu.SMEM)] + [spec] * len(arrays),
        out_specs=[spec] * len(shapes),
        compiler_params=pltpu.CompilerParams(vmem_limit_bytes=VMEM_LIMIT),
        cost_estimate=pl.CostEstimate(flops=0, bytes_accessed=LOCAL_BYTES, transcendentals=0),
    )(flags, *arrays)


def pack(shards, g):
    rows, width = shards[0].shape[0], shards[0].shape[1] // (GROUP * CORES)
    count = len(shards)

    def kernel(flags, *refs):
        sources, targets = refs[:count], refs[count:]
        for by in range(GROUP):
            to = lax.rem(flags[0] + by, GROUP)
            for core in range(CORES):
                start = pl.multiple_of((to * CORES + core) * width, width)
                for number in range(count):
                    at = (core * count + number) * width
                    targets[by][:, at : at + width] = sources[number][:, pl.ds(start, width)]

    shape = jax.ShapeDtypeStruct((rows, CORES * count * width), shards[0].dtype)
    return vmem_call(kernel, [shape] * GROUP, [g], shards)


def sort(pieces, g, c):
    rows, half = pieces[0].shape[0], pieces[0].shape[1] // CORES

    def kernel(flags, *refs):
        sources, targets = refs[:GROUP], refs[GROUP:]
        for by in range(GROUP):
            row = pl.multiple_of(lax.rem(flags[0] + GROUP - by, GROUP) * rows, rows)
            for number in range(CORES):
                core = flags[1] if number == 0 else 1 - flags[1]
                targets[number][pl.ds(row, rows), :] = sources[by][
                    :, pl.ds(pl.multiple_of(core * half, half), half)
                ]

    shape = jax.ShapeDtypeStruct((GROUP * rows, half), pieces[0].dtype)
    return vmem_call(kernel, [shape] * CORES, [g, c], pieces)


def unpack(pieces, g, count):
    rows, width = pieces[0].shape[0], pieces[0].shape[1] // (CORES * count)

    def kernel(flags, *refs):
        sources, targets = refs[:GROUP], refs[GROUP:]
        for by in range(GROUP):
            source = lax.rem(flags[0] + GROUP - by, GROUP)
            for core in range(CORES):
                start = pl.multiple_of((source * CORES + core) * width, width)
                for number in range(count):
                    at = (core * count + number) * width
                    targets[number][:, pl.ds(start, width)] = sources[by][
                        :, at : at + width
                    ].astype(F32)

    shape = jax.ShapeDtypeStruct((rows, GROUP * CORES * width), F32)
    return vmem_call(kernel, [shape] * count, [g], pieces)


def by_core(mine, got, c):
    rows = mine.shape[0]

    def kernel(flags, first, second, target):
        target[pl.ds(pl.multiple_of(flags[0] * rows, rows), rows), :] = first[...]
        target[pl.ds(pl.multiple_of((1 - flags[0]) * rows, rows), rows), :] = second[...]

    [out] = vmem_call(
        kernel,
        [jax.ShapeDtypeStruct((CORES * rows, mine.shape[1]), mine.dtype)],
        [c],
        [mine, got],
    )
    return out


def deal(mine, got, g, c):
    rows, width = mine.shape[0] // GROUP, mine.shape[1]

    def kernel(flags, first, second, *targets):
        for by in range(GROUP):
            row = pl.multiple_of(lax.rem(flags[0] + by, GROUP) * rows, rows)
            for number, source in enumerate((first, second)):
                core = flags[1] if number == 0 else 1 - flags[1]
                at = pl.ds(pl.multiple_of(core * width, width), width)
                targets[by][:, at] = source[pl.ds(row, rows), :]

    shape = jax.ShapeDtypeStruct((rows, CORES * width), mine.dtype)
    return vmem_call(kernel, [shape] * GROUP, [g, c], [mine, got])


def weight_grads(factors, reps, cuts):
    step = 256
    count = factors[0][0].shape[0]
    total = sum(cuts)
    starts = [sum(cuts[:number]) for number in range(len(cuts))]

    def products(lefts, rights, own, other):
        for left, right, start, width in zip(lefts, rights, starts, cuts):
            product = mm(left[...], right[...], TN).astype(BF16)
            own[:, start : start + width] = product[:, :width]
            other[:, start : start + width] = product[:, width:]

    lefts = [left for left, _ in factors]
    rights = [right for _, right in factors]
    size = len(factors)
    whole = [pl.BlockSpec(v.shape, lambda i: (0, 0)) for v in rights]
    params = {
        "compiler_params": pltpu.CompilerParams(vmem_limit_bytes=VMEM_LIMIT),
        "cost_estimate": pl.CostEstimate(flops=0, bytes_accessed=LOCAL_BYTES, transcendentals=0),
    }
    if reps != 2:

        def kernel(*refs):
            products(refs[:size], refs[size : 2 * size], *refs[2 * size :])

        out = pl.BlockSpec((step, total), lambda i: (i, 0))
        return pl.pallas_call(
            kernel,
            grid=(D // step,),
            in_specs=[pl.BlockSpec((count, step), lambda i: (0, i))] * size + whole,
            out_specs=[out, out],
            out_shape=[jax.ShapeDtypeStruct((D, total), BF16)] * 2,
            **params,
        )(*lefts, *rights)

    steps = D // 2 // step
    half = steps // 2

    def kernel(*refs):
        upper, lower, right = refs[:size], refs[size : 2 * size], refs[2 * size : 3 * size]
        to_q, to_x, beside_top, below_low, keep = refs[3 * size :]

        @pl.when(pl.program_id(0) < half)
        def _():
            products(upper, right, keep, beside_top)
            products(lower, right, to_q.at[1], to_q.at[0])

        @pl.when(pl.program_id(0) >= half)
        def _():
            products(upper, right, keep, to_x.at[1])
            products(lower, right, below_low, to_x.at[0])

    first = lambda i: jnp.minimum(i, half - 1)
    last = lambda i: jnp.maximum(i - half, 0)
    rows = D // 4
    return pl.pallas_call(
        kernel,
        grid=(steps,),
        in_specs=[pl.BlockSpec((count, step), lambda i: (0, i))] * size
        + [pl.BlockSpec((count, step), lambda i: (0, i + steps))] * size
        + whole,
        out_specs=[
            pl.BlockSpec((2, step, total), lambda i: (0, first(i), 0)),
            pl.BlockSpec((2, step, total), lambda i: (0, last(i), 0)),
            pl.BlockSpec((step, total), lambda i: (first(i), 0)),
            pl.BlockSpec((step, total), lambda i: (last(i), 0)),
            pl.BlockSpec((step, total), lambda i: (i, 0)),
        ],
        out_shape=[
            jax.ShapeDtypeStruct(shape, BF16)
            for shape in (
                (2, rows, total), (2, rows, total), (rows, total), (rows, total), (2 * rows, total)
            )
        ],
        **params,
    )(*lefts, *lefts, *rights)


NN, NT, TN = ((1,), (0,)), ((1,), (1,)), ((0,), (0,))
VMEM_LIMIT = 60 << 20
LOCAL_BYTES = 200 << 20
HEADS_HERE = 2
ROWS = 2
LENGTH = 128
ROOT = HEAD_DIM ** (-0.5)


def mm(a, b, dims=NN):
    return lax.dot_general(a, b, (dims, ((), ())), preferred_element_type=F32)


def eye(size):
    return lax.broadcasted_iota(jnp.int32, (size, size), 0) == lax.broadcasted_iota(
        jnp.int32, (size, size), 1
    )


def to_column(row):
    return jnp.sum(jnp.where(eye(row.shape[1]), row, 0.0), axis=1, keepdims=True)


def to_row(column):
    return jnp.sum(jnp.where(eye(column.shape[0]), column, 0.0), axis=0, keepdims=True)


def head(values, kind, number):
    start = (number * 3 + kind) * HEAD_DIM
    return values[:, start : start + HEAD_DIM]


def pair(values, number):
    return values[:, number * HEAD_DIM : (number + 1) * HEAD_DIM]


def rotated(values, cosine, sine):
    return values * cosine + pltpu.roll(values, HEAD_DIM // 2, 1) * sine


def allowed_keys(segment_row):
    size = segment_row.shape[1]
    same = to_column(segment_row) == segment_row
    later = lax.broadcasted_iota(jnp.int32, (size, size), 1) > lax.broadcasted_iota(
        jnp.int32, (size, size), 0
    )
    return jnp.logical_and(same, jnp.logical_not(later))


def softmax_of(query, key, allowed):
    scores = jnp.where(allowed, mm(query, key, NT) * ROOT, -1e30)
    expo = jnp.exp(scores - jnp.max(scores, axis=1, keepdims=True))
    return expo / jnp.sum(expo, axis=1, keepdims=True)


def scale_of(squares, kind):
    return to_column(lax.rsqrt(squares[kind : kind + 1] / D + EPSILON))


def row_call(kernel, rows, ins, outs):
    def spec(shape, block):
        if block == "whole":
            return pl.BlockSpec(shape, lambda i: (0,) * len(shape))
        return pl.BlockSpec((ROWS * block,) + shape[1:], lambda i: (i,) + (0,) * (len(shape) - 1))

    return pl.pallas_call(
        kernel,
        grid=(rows // ROWS,),
        in_specs=[spec(v.shape, block) for v, block in ins],
        out_specs=[spec(shape, block) for shape, _, block in outs],
        out_shape=[jax.ShapeDtypeStruct(shape, dtype) for shape, dtype, _ in outs],
        compiler_params=pltpu.CompilerParams(vmem_limit_bytes=VMEM_LIMIT),
        cost_estimate=pl.CostEstimate(flops=0, bytes_accessed=0, transcendentals=0),
    )(*[v for v, _ in ins])


def row_views(row, *refs):
    return [ref.at[row * LENGTH : (row + 1) * LENGTH] for ref in refs]


def project_kernel(tokens, weights, out, squares):
    out[...] = mm(tokens[...], weights[...])
    for row in range(ROWS):
        [product] = row_views(row, out)
        for kind in range(2):
            total = 0.0
            for number in range(HEADS_HERE):
                part = head(product, kind, number)
                total = total + jnp.sum(part * part, axis=1, keepdims=True)
            squares[row, kind : kind + 1] = to_row(total)


def attend_kernel(
    qkv_all, squares, gains, cosine_all, sine_all, segments, weights,
    query_all, key_all, value_all, mixed_all, out,
):
    for row in range(ROWS):
        qkv, cosine, sine, query_out, key_out, value_out, mixed = row_views(
            row, qkv_all, cosine_all, sine_all, query_all, key_all, value_all, mixed_all
        )
        allowed = allowed_keys(segments[row])
        scales = [scale_of(squares[row], kind) for kind in range(2)]
        for number in range(HEADS_HERE):
            low = [
                rotated(
                    head(qkv, kind, number) * scales[kind] * gains[kind, number : number + 1],
                    cosine[...],
                    sine[...],
                ).astype(BF16)
                for kind in range(2)
            ]
            value = head(qkv, 2, number).astype(BF16)
            probs = softmax_of(*low, allowed).astype(BF16)
            where = slice(number * HEAD_DIM, (number + 1) * HEAD_DIM)
            query_out[:, where] = low[0]
            key_out[:, where] = low[1]
            value_out[:, where] = value
            mixed[:, where] = mm(probs, value).astype(BF16)
    out[...] = mm(mixed_all[...], weights[...], NT).astype(BF16)


def attend_back_kernel(
    grads, weights, query_all, key_all, value_all, qkv_all, squares, gains, cosine_all, sine_all,
    segments, weighted_all, value_grad_all, inner, gain_grad,
):
    @pl.when(pl.program_id(0) == 0)
    def _():
        gain_grad[...] = jnp.zeros_like(gain_grad)

    mixed_grads = mm(grads[...], weights[...]).astype(BF16)
    for row in range(ROWS):
        queries, keys, values, qkv, cosine, sine, weighted, value_grad = row_views(
            row, query_all, key_all, value_all, qkv_all, cosine_all, sine_all, weighted_all,
            value_grad_all,
        )
        allowed = allowed_keys(segments[row])
        scales = [scale_of(squares[row], kind) for kind in range(2)]
        sums = [0.0, 0.0]
        for number in range(HEADS_HERE):
            query, key, value = pair(queries, number), pair(keys, number), pair(values, number)
            mixed_grad = pair(mixed_grads[row * LENGTH : (row + 1) * LENGTH], number)
            probs = softmax_of(query, key, allowed)
            where = slice(number * HEAD_DIM, (number + 1) * HEAD_DIM)
            value_grad[:, where] = mm(probs.astype(BF16), mixed_grad, TN).astype(BF16)
            prob_grad = mm(mixed_grad, value, NT)
            score_grad = probs * (prob_grad - jnp.sum(probs * prob_grad, axis=1, keepdims=True))
            score_low = (score_grad * ROOT).astype(BF16)
            turned = (mm(score_low, key), mm(score_low, query, TN))
            for kind in range(2):
                normed = rotated(turned[kind], cosine[...], -sine[...])
                part = head(qkv, kind, number)
                gain_grad[kind, number : number + 1] += jnp.sum(
                    normed * part * scales[kind], axis=0, keepdims=True
                )
                normed = normed * gains[kind, number : number + 1]
                sums[kind] = sums[kind] + jnp.sum(part * normed, axis=1, keepdims=True)
                start = (kind * HEADS_HERE + number) * HEAD_DIM
                weighted[:, start : start + HEAD_DIM] = normed
        for kind in range(2):
            inner[row, kind : kind + 1] = to_row(sums[kind])


def input_grad_kernel(
    weighted_all, qkv_all, squares, inner, value_grad_all, weights, qkv_grad_all, out
):
    for row in range(ROWS):
        weighted, qkv, value_grad, qkv_grad = row_views(
            row, weighted_all, qkv_all, value_grad_all, qkv_grad_all
        )
        for kind in range(2):
            scale = scale_of(squares[row], kind)
            shift_by = scale * scale * scale * (to_column(inner[row][kind : kind + 1]) / D)
            for number in range(HEADS_HERE):
                start = (kind * HEADS_HERE + number) * HEAD_DIM
                part = weighted[:, start : start + HEAD_DIM]
                start = (number * 3 + kind) * HEAD_DIM
                qkv_grad[:, start : start + HEAD_DIM] = (
                    scale * part - head(qkv, kind, number) * shift_by
                ).astype(BF16)
        for number in range(HEADS_HERE):
            start = (number * 3 + 2) * HEAD_DIM
            qkv_grad[:, start : start + HEAD_DIM] = pair(value_grad, number)
    out[...] = mm(qkv_grad_all[...], weights[...], NT).astype(BF16)


class Place:
    def __init__(self, reps):
        self.reps = reps
        self.g = lax.axis_index("g")
        self.q = lax.axis_index("q")
        self.c = lax.axis_index("c")
        self.x = lax.axis_index("x")

    def orders(self):
        return [
            [
                (g * self.reps + (q ^ flip)) * CORES + c
                for q in range(self.reps)
                for c in range(CORES)
                for g in range(GROUP)
            ]
            for flip in ((0, 1) if self.reps == 2 else (0,))
        ]

    def shuffle(self, value, orders):
        if self.reps == 2:
            return reorder(value, self.q, orders)
        rows, size = value.shape[0], D // len(orders[0])
        blocks = value.reshape(rows, -1, size)
        return jnp.stack([blocks[:, i] for i in orders[0]], 1).reshape(rows, D)

    def to_local(self, value):
        return self.shuffle(value, self.orders())

    def to_global(self, value):
        return self.shuffle(
            value, [[order.index(i) for i in range(len(order))] for order in self.orders()]
        )

    def send(self, pieces):
        return [pieces[0]] + [shift(pieces[by], by) for by in range(1, GROUP)]

    def spread(self, shards):
        return self.send(pack(shards, self.g))

    def settle(self, pieces):
        mine, other = sort(pieces, self.g, self.c)
        return [mine, swap(other, "c")]

    def settled(self, halves):
        return by_core(*halves, self.c)

    def widen(self, held):
        if self.reps != 2:
            return [lax.all_gather(held, "q", axis=0, tiled=True)]
        return [held, swap(held, "q"), swap(held, "x")]

    def widened(self, blocks):
        if self.reps != 2:
            return [*blocks, swap(blocks[0], "x")]
        half = blocks[0].shape[0] // 2
        return [*blocks, swap(blocks[2][:half], "q"), swap(blocks[1][half:], "x")]

    def join(self, blocks, cuts):
        rows = blocks[0].shape[0]
        spots = [(0, 0), (0, 1)]
        if self.reps == 2:
            spots = [(0, 0), (rows, 0), (0, 1), (rows, 1), (rows + rows // 2, 1)]
        moves, shapes = [], [(D, 2 * (stop - start)) for start, stop in cuts]
        for number, (start, stop) in enumerate(cuts):
            for at, (row, side) in enumerate(spots):
                moves.append((at, (start, stop), number, row, side * (stop - start)))
        return assemble(blocks, moves, shapes)

    def narrow(self, parts):
        if self.reps != 2:
            return [swap(parts[1], "x")]
        return [swap(parts[0], "q"), swap(parts[1], "x")]

    def narrow_next(self, parts, came):
        if self.reps != 2:
            total = add(parts[0], came[0])
            return [lax.psum_scatter(total, "q", scatter_dimension=0, tiled=True)]
        _, _, beside_top, below_low, _ = parts
        return [swap(add(beside_top, came[0][0]), "x"), swap(add(below_low, came[1][0]), "q")]

    def narrowed(self, parts, came, more):
        if self.reps != 2:
            return jnp.split(more[0], 2)
        half = parts[4].shape[0] // 2
        return (
            add(parts[4][:half], more[0], came[0][1]),
            add(parts[4][half:], came[1][1], more[1]),
        )

    def unsettle(self, halves):
        top, low = halves
        mine, other = jnp.where(self.c == 0, top, low), jnp.where(self.c == 0, low, top)
        return [mine, swap(other, "c")]

    def collect(self, halves):
        return self.send(deal(*halves, self.g, self.c))


def rope_tables(segments):
    places = jnp.arange(segments.shape[1], dtype=jnp.int32)
    same = segments[:, :, None] == segments[:, None, :]
    earlier = same & (places[None, None, :] < places[None, :, None])
    spot = jnp.sum(earlier.astype(jnp.int32), axis=2).astype(F32)
    halfway = HEAD_DIM // 2
    inverse = jnp.exp(jnp.arange(halfway, dtype=F32) * (-2.0 * math.log(ROPE_BASE) / HEAD_DIM))
    angles = spot.reshape(-1, 1) * inverse
    cosine, sine = jnp.cos(angles), jnp.sin(angles)
    return jnp.concatenate([cosine, cosine], 1), jnp.concatenate([-sine, sine], 1)


def norm_scale(values):
    return lax.rsqrt(jnp.mean(values * values, axis=-1, keepdims=True) + EPSILON)


def norm_back(values, scale, gain, grad):
    weighted = grad * gain
    inner = jnp.sum(values * weighted, axis=-1, keepdims=True) / D
    return (
        scale * weighted - values * (scale * scale * scale) * inner,
        jnp.sum(grad * values * scale, axis=0),
    )


def on_device(
    reps,
    tokens,
    segment_ids,
    query_proj,
    key_proj,
    value_proj,
    out_proj,
    query_gain,
    key_gain,
    attn_gain,
    gate_proj,
    up_proj,
    down_proj,
    mlp_gain,
    cotangent,
):
    place = Place(reps)
    slots = GROUP * CORES
    shard_rows = query_proj.shape[0]
    length = tokens.shape[2]
    slot = place.g * CORES + place.c

    step = Order()
    count = slots * length
    cut = 3 * HEAD_DIM

    def team_scatter(value):
        return lax.psum_scatter(value, TEAM, scatter_dimension=0, tiled=True)

    def team_gather(value):
        return lax.all_gather(value, TEAM, axis=0, tiled=True)

    def team_sum(value):
        value = value + step(swap(value, "c"))
        for by in (1, 2):
            value = value + step(
                lax.ppermute(value, "g", [(i, i ^ by) for i in range(GROUP)])
            )
        return value

    attn = place.spread([query_proj, key_proj, value_proj, out_proj])
    own_row = place.to_local(pick(tokens, place.x, 0)[0])
    segments = pick(segment_ids, place.x, 0)
    segments = ordered(place.c, segments, swap(segments, "c"), 0)[:, 0]
    gate = pack([gate_proj], place.g)
    feed = pack([up_proj, down_proj], place.g)
    attn, own_row, segments, gate, feed = step(attn, own_row, segments, gate, feed)
    all_rows = team_gather(own_row)
    segments = [segments] + [shift(segments, by) for by in range(1, GROUP)]
    attn = step(place.settle(attn))
    attn = place.widen(place.settled(attn))
    gains = jnp.stack([pick(w.reshape(slots, HEAD_DIM), slot, 0) for w in (query_gain, key_gain)])
    gains = jnp.stack([gains, swap(gains, "x")], 1)
    gathered = jnp.zeros((GROUP,) + segments[0].shape, segments[0].dtype)
    for by, piece in enumerate(segments):
        gathered = put(gathered, piece, (place.g - by) % GROUP)
    segments = gathered.reshape(slots, length)
    cosine, sine = rope_tables(segments)
    segments = segments.astype(F32)[:, None]
    attn, gains, segments, gate = step(attn, gains, segments, gate)
    gate = place.send(gate)
    attn = step(place.widened(attn))
    qkv_full, out_full = step(place.join(attn, [(0, cut), (cut, 4 * HEAD_DIM)]))
    all_rows, cosine, sine = step(all_rows, cosine, sine)

    qkv, squares = step(
        *row_call(
            project_kernel,
            slots,
            [(all_rows, length), (qkv_full, "whole")],
            [((count, 6 * HEAD_DIM), F32, length), ((slots, 2, length), F32, 1)],
        )
    )
    gate = step(place.settle(step(gate)))
    gate = place.widen(place.settled(gate))
    squares = team_sum(squares)
    squares, feed = step(squares, feed)
    feed = place.send(feed)
    low = ((count, 2 * HEAD_DIM), BF16, length)
    query_low, key_low, value_low, mixed, attn_part, gate = step(
        *row_call(
            attend_kernel,
            slots,
            [
                (qkv, length),
                (squares, 1),
                (gains, "whole"),
                (cosine, length),
                (sine, length),
                (segments, 1),
                (out_full, "whole"),
            ],
            [low, low, low, low, ((count, D), BF16, length)],
        ),
        gate,
    )
    gate = place.widened(gate)
    attn_part, gate, feed = step(attn_part, gate, feed)
    projected = team_scatter(attn_part)
    feed = place.settle(feed)
    feed = place.widen(place.settled(step(feed)))
    width = gate_proj.shape[1] // slots
    feed = step(feed)
    projected = step(projected)
    projected = projected.astype(F32)
    attn_gain, mlp_gain = place.to_local(jnp.stack([attn_gain, mlp_gain]))
    projected_scale = norm_scale(projected)
    hidden = own_row.astype(F32) + projected * projected_scale * attn_gain
    hidden_low, hidden = step(hidden.astype(BF16), hidden)
    hidden_all = team_gather(hidden_low)
    [gate_full] = step(place.join(gate, [(0, width)]))
    feed = place.widened(feed)
    up_full, down_full = place.join(step(feed), [(0, width), (width, 2 * width)])
    own_cotangent = place.to_local(pick(cotangent, place.x, 0)[0]).astype(F32)
    hidden_all, gate_full, up_full, down_full, own_cotangent = step(
        hidden_all, gate_full, up_full, down_full, own_cotangent
    )

    lifted = dot(hidden_all, up_full)
    gated = dot(hidden_all, gate_full)
    active = (gated / (1.0 + jnp.exp(-gated)) * lifted).astype(BF16)
    reduced = team_scatter(step(dot_nt(active, down_full).astype(BF16)))
    reduced = step(reduced).astype(F32)
    reduced_scale = norm_scale(reduced)
    reduced_grad, mlp_gain_grad = norm_back(reduced, reduced_scale, mlp_gain, own_cotangent)
    reduced_all = team_gather(step(reduced_grad.astype(BF16)))
    own_out = place.to_global((hidden + reduced * reduced_scale * mlp_gain).astype(BF16))
    layer_out = ordered(place.x, own_out, swap(own_out, "x"), 0)[:, None]
    reduced_all, mlp_gain_grad, layer_out = step(reduced_all, mlp_gain_grad, layer_out)

    active_grad = dot(reduced_all, down_full)
    gate_sigmoid = 1.0 / (1.0 + jnp.exp(-gated))
    gated_grad = (
        active_grad * lifted * gate_sigmoid * (1.0 + gated * (1.0 - gate_sigmoid))
    ).astype(BF16)
    lifted_grad = (active_grad * gated * gate_sigmoid).astype(BF16)
    hidden_part = dot_nt(gated_grad, gate_full) + dot_nt(lifted_grad, up_full)
    hidden_part, gated_grad, lifted_grad = step(hidden_part.astype(BF16), gated_grad, lifted_grad)
    hidden_part = team_scatter(hidden_part)
    down = step(weight_grads([(reduced_all, active)], reps, [width]))
    down_came = place.narrow(down)
    feed = step(
        weight_grads([(hidden_all, gated_grad), (hidden_all, lifted_grad)], reps, [width, width])
    )
    down_came = step(down_came)
    down_more = place.narrow_next(down, down_came)
    hidden_grad = own_cotangent + step(hidden_part).astype(F32)
    projected_grad, attn_gain_grad = norm_back(projected, projected_scale, attn_gain, hidden_grad)
    projected_low, hidden_grad, attn_gain_grad = step(
        projected_grad.astype(BF16), hidden_grad, attn_gain_grad
    )
    projected_all = team_gather(projected_low)
    down_more, feed = step(down_more, feed)
    feed_came = place.narrow(feed)
    down = step(place.unsettle(place.narrowed(down, down_came, down_more)))
    norm_gain_grads = place.to_global(jnp.stack([attn_gain_grad, mlp_gain_grad]))
    down = deal(*down, place.g, place.c)
    norm_gain_grads, down = step(norm_gain_grads, down)

    projected_all, down = step(projected_all, down)
    down = place.send(down)
    weighted, value_grad, inner, head_gain_grads, down, feed_came = step(
        *row_call(
            attend_back_kernel,
            slots,
            [
                (projected_all, length),
                (out_full, "whole"),
                (query_low, length),
                (key_low, length),
                (value_low, length),
                (qkv, length),
                (squares, 1),
                (gains, "whole"),
                (cosine, length),
                (sine, length),
                (segments, 1),
            ],
            [
                ((count, 4 * HEAD_DIM), F32, length),
                low,
                ((slots, 2, length), F32, 1),
                (gains.shape, F32, "whole"),
            ],
        ),
        down,
        feed_came,
    )
    spots = jnp.zeros((2, 2, slots, HEAD_DIM), F32)
    for number in range(2):
        spots = lax.dynamic_update_slice(
            spots,
            head_gain_grads[:, number][:, None, None],
            (0, place.x if number == 0 else 1 - place.x, slot, 0),
        )
    message = jnp.concatenate([v.reshape(-1, HEAD_DIM) for v in (inner, spots, norm_gain_grads)])
    feed_more = place.narrow_next(feed, feed_came)
    message = team_sum(message)
    inner, gain_grads = message[: 2 * slots].reshape(inner.shape), message[2 * slots :]
    gain_x = swap(gain_grads, "x")
    qkv_grad, input_part, feed_more, gain_x = step(
        *row_call(
            input_grad_kernel,
            slots,
            [
                (weighted, length),
                (qkv, length),
                (squares, 1),
                (inner, 1),
                (value_grad, length),
                (qkv_full, "whole"),
            ],
            [((count, 6 * HEAD_DIM), BF16, length), ((count, D), BF16, length)],
        ),
        feed_more,
        gain_x,
    )
    input_part = team_scatter(input_part)
    attn = step(
        weight_grads([(all_rows, qkv_grad), (projected_all, mixed)], reps, [cut, HEAD_DIM])
    )
    attn_came = place.narrow(attn)
    feed = step(place.unsettle(place.narrowed(feed, feed_came, feed_more)))
    feed = place.send(step(deal(*feed, place.g, place.c)))
    gain_grads = gain_grads + gain_x
    gain_q = swap(gain_grads, "q") if reps == 2 else lax.psum(gain_grads, "q") - gain_grads
    [down_grad] = step(unpack(down, place.g, 1))
    attn_came = step(attn_came)
    attn_more = place.narrow_next(attn, attn_came)
    input_part = step(input_part)
    own_grad = place.to_global((hidden_grad + input_part.astype(F32)).astype(BF16))
    own_grad_x = swap(step(own_grad), "x")
    feed = step(feed)
    attn_more = step(attn_more)
    attn = place.unsettle(place.narrowed(attn, attn_came, attn_more))
    attn, gain_q = step(attn, gain_q)
    attn = place.send(step(deal(*attn, place.g, place.c)))
    attn[1], feed, own_grad_x = step(attn[1], feed, own_grad_x)
    gate_grad, up_grad = unpack(feed, place.g, 2)
    summed = (gain_grads + gain_q).reshape(4, D)
    tokens_grad = ordered(place.x, own_grad, own_grad_x, 0)[:, None].astype(F32)
    tokens_grad, gate_grad, up_grad, summed = step(tokens_grad, gate_grad, up_grad, summed)
    attn_grads = unpack(step(attn), place.g, 4)
    summed = summed + step.token
    half_of = lambda v: pick(v.reshape(2, -1), place.x, 0)
    return (
        layer_out,
        tokens_grad,
        *attn_grads,
        half_of(summed[0]),
        half_of(summed[1]),
        summed[2],
        gate_grad,
        up_grad,
        down_grad,
        summed[3],
    )


def solution(mesh):
    reps = mesh.shape["dp"] // (GROUP * CORES)
    folded = Mesh(
        mesh.devices.reshape(GROUP, reps, CORES, mesh.shape["tensor"]), ("g", "q", "c", "x")
    )
    dp = ("g", "q", "c")
    row = P(None, dp, None, None)
    weight = P(dp, "x")
    gain = P("x")
    in_specs = (row, P(None, dp, None)) + (weight,) * 4 + (gain, gain, P()) + (weight,) * 3
    in_specs += (P(), row)
    out_specs = (row, row) + (weight,) * 4 + (gain, gain, P()) + (weight,) * 3 + (P(),)

    def body(*args):
        return on_device(reps, *args)

    return jax.shard_map(
        body, mesh=folded, in_specs=in_specs, out_specs=out_specs, check_vma=False
    )
```

```python
import math

import jax
import jax.numpy as jnp
from jax import lax
from jax.experimental import pallas as pl
from jax.experimental.pallas import tpu as pltpu
from jax.sharding import Mesh, PartitionSpec as P

D = 2048
HEAD_DIM = 128
EPSILON = 1e-06
ROPE_BASE = 500000.0
GROUP = 4
CORES = 2
F32 = jnp.float32
BF16 = jnp.bfloat16
TEAM = ("g", "c")


def dot(a, b):
    return jnp.dot(a, b, preferred_element_type=F32)


def dot_nt(a, b):
    return lax.dot_general(a, b, (((1,), (1,)), ((), ())), preferred_element_type=F32)


def dot_tn(a, b):
    return lax.dot_general(a, b, (((0,), (0,)), ((), ())), preferred_element_type=F32)


def swap(value, axis):
    return lax.ppermute(value, axis, [(0, 1), (1, 0)])


def shift(value, by):
    return lax.ppermute(value, "g", [(i, (i + by) % GROUP) for i in range(GROUP)])


def pick(value, index, axis):
    return lax.dynamic_index_in_dim(value, index, axis, keepdims=False)


def put(value, piece, index, axis=0):
    return lax.dynamic_update_index_in_dim(value, piece, index, axis)


def ordered(flag, first, second, axis):
    return jnp.where(
        flag == 0, jnp.stack([first, second], axis), jnp.stack([second, first], axis)
    )


def add(*values):
    return sum(v.astype(F32) for v in values).astype(BF16)


class Order:
    def __init__(self):
        self.token = jnp.zeros((), F32)

    def __call__(self, *values):
        *values, self.token = lax.optimization_barrier((*values, self.token))
        return values[0] if len(values) == 1 else values


def assemble(pieces, moves, shapes):
    def kernel(*refs):
        sources, (*targets, sems) = refs[: len(pieces)], refs[len(pieces) :]
        copies = []
        for number, (source, columns, target, row, column) in enumerate(moves):
            rows, width = pieces[source].shape[0], columns[1] - columns[0]
            copies.append(
                pltpu.make_async_copy(
                    sources[source].at[:, pl.ds(columns[0], width)],
                    targets[target].at[pl.ds(row, rows), pl.ds(column, width)],
                    sems.at[number],
                )
            )
        for copy in copies:
            copy.start()
        for copy in copies:
            copy.wait()

    out = pl.pallas_call(
        kernel,
        out_shape=[jax.ShapeDtypeStruct(shape, pieces[0].dtype) for shape in shapes],
        in_specs=[pl.BlockSpec(memory_space=pl.ANY)] * len(pieces),
        out_specs=[pl.BlockSpec(memory_space=pltpu.VMEM)] * len(shapes),
        scratch_shapes=[pltpu.SemaphoreType.DMA((len(moves),))],
        compiler_params=pltpu.CompilerParams(vmem_limit_bytes=24 << 20),
        cost_estimate=pl.CostEstimate(
            flops=0,
            bytes_accessed=sum(4 * math.prod(shape) for shape in shapes),
            transcendentals=0,
        ),
    )(*pieces)
    return out


def reorder(values, flag, orders):
    size = values.shape[1] // len(orders[0])

    def kernel(flag_ref, source, target):
        for number, order in enumerate(orders):

            @pl.when(flag_ref[0] == number)
            def _():
                for to, block in enumerate(order):
                    target[:, to * size : (to + 1) * size] = source[
                        :, block * size : (block + 1) * size
                    ]

    return pl.pallas_call(
        kernel,
        out_shape=jax.ShapeDtypeStruct(values.shape, values.dtype),
        in_specs=[
            pl.BlockSpec(memory_space=pltpu.SMEM),
            pl.BlockSpec(memory_space=pltpu.VMEM),
        ],
        out_specs=pl.BlockSpec(memory_space=pltpu.VMEM),
        cost_estimate=pl.CostEstimate(
            flops=0, bytes_accessed=4 * values.size, transcendentals=0
        ),
    )(jnp.reshape(flag, (1,)).astype(jnp.int32), values)


def vmem_call(kernel, shapes, scalars, arrays):
    flags = jnp.stack([jnp.asarray(v, jnp.int32) for v in scalars])
    spec = pl.BlockSpec(memory_space=pltpu.VMEM)
    return pl.pallas_call(
        kernel,
        out_shape=shapes,
        in_specs=[pl.BlockSpec(memory_space=pltpu.SMEM)] + [spec] * len(arrays),
        out_specs=[spec] * len(shapes),
        compiler_params=pltpu.CompilerParams(vmem_limit_bytes=VMEM_LIMIT),
        cost_estimate=pl.CostEstimate(flops=0, bytes_accessed=LOCAL_BYTES, transcendentals=0),
    )(flags, *arrays)


def pack(shards, g):
    rows, width = shards[0].shape[0], shards[0].shape[1] // (GROUP * CORES)
    count = len(shards)

    def kernel(flags, *refs):
        sources, targets = refs[:count], refs[count:]
        for by in range(GROUP):
            to = lax.rem(flags[0] + by, GROUP)
            for core in range(CORES):
                start = pl.multiple_of((to * CORES + core) * width, width)
                for number in range(count):
                    at = (core * count + number) * width
                    targets[by][:, at : at + width] = sources[number][:, pl.ds(start, width)]

    shape = jax.ShapeDtypeStruct((rows, CORES * count * width), shards[0].dtype)
    return vmem_call(kernel, [shape] * GROUP, [g], shards)


def sort(pieces, g, c):
    rows, half = pieces[0].shape[0], pieces[0].shape[1] // CORES

    def kernel(flags, *refs):
        sources, targets = refs[:GROUP], refs[GROUP:]
        for by in range(GROUP):
            row = pl.multiple_of(lax.rem(flags[0] + GROUP - by, GROUP) * rows, rows)
            for number in range(CORES):
                core = flags[1] if number == 0 else 1 - flags[1]
                targets[number][pl.ds(row, rows), :] = sources[by][
                    :, pl.ds(pl.multiple_of(core * half, half), half)
                ]

    shape = jax.ShapeDtypeStruct((GROUP * rows, half), pieces[0].dtype)
    return vmem_call(kernel, [shape] * CORES, [g, c], pieces)


def unpack(pieces, g, count):
    rows, width = pieces[0].shape[0], pieces[0].shape[1] // (CORES * count)

    def kernel(flags, *refs):
        sources, targets = refs[:GROUP], refs[GROUP:]
        for by in range(GROUP):
            source = lax.rem(flags[0] + GROUP - by, GROUP)
            for core in range(CORES):
                start = pl.multiple_of((source * CORES + core) * width, width)
                for number in range(count):
                    at = (core * count + number) * width
                    targets[number][:, pl.ds(start, width)] = sources[by][
                        :, at : at + width
                    ].astype(F32)

    shape = jax.ShapeDtypeStruct((rows, GROUP * CORES * width), F32)
    return vmem_call(kernel, [shape] * count, [g], pieces)


def by_core(mine, got, c):
    rows = mine.shape[0]

    def kernel(flags, first, second, target):
        target[pl.ds(pl.multiple_of(flags[0] * rows, rows), rows), :] = first[...]
        target[pl.ds(pl.multiple_of((1 - flags[0]) * rows, rows), rows), :] = second[...]

    [out] = vmem_call(
        kernel,
        [jax.ShapeDtypeStruct((CORES * rows, mine.shape[1]), mine.dtype)],
        [c],
        [mine, got],
    )
    return out


def deal(mine, got, g, c):
    rows, width = mine.shape[0] // GROUP, mine.shape[1]

    def kernel(flags, first, second, *targets):
        for by in range(GROUP):
            row = pl.multiple_of(lax.rem(flags[0] + by, GROUP) * rows, rows)
            for number, source in enumerate((first, second)):
                core = flags[1] if number == 0 else 1 - flags[1]
                at = pl.ds(pl.multiple_of(core * width, width), width)
                targets[by][:, at] = source[pl.ds(row, rows), :]

    shape = jax.ShapeDtypeStruct((rows, CORES * width), mine.dtype)
    return vmem_call(kernel, [shape] * GROUP, [g, c], [mine, got])


def weight_grads(factors, reps, cuts):
    step = 256
    count = factors[0][0].shape[0]
    total = sum(cuts)
    starts = [sum(cuts[:number]) for number in range(len(cuts))]

    def products(lefts, rights, own, other):
        for left, right, start, width in zip(lefts, rights, starts, cuts):
            product = mm(left[...], right[...], TN).astype(BF16)
            own[:, start : start + width] = product[:, :width]
            other[:, start : start + width] = product[:, width:]

    lefts = [left for left, _ in factors]
    rights = [right for _, right in factors]
    size = len(factors)
    whole = [pl.BlockSpec(v.shape, lambda i: (0, 0)) for v in rights]
    params = {
        "compiler_params": pltpu.CompilerParams(vmem_limit_bytes=VMEM_LIMIT),
        "cost_estimate": pl.CostEstimate(flops=0, bytes_accessed=LOCAL_BYTES, transcendentals=0),
    }
    if reps != 2:

        def kernel(*refs):
            products(refs[:size], refs[size : 2 * size], *refs[2 * size :])

        out = pl.BlockSpec((step, total), lambda i: (i, 0))
        return pl.pallas_call(
            kernel,
            grid=(D // step,),
            in_specs=[pl.BlockSpec((count, step), lambda i: (0, i))] * size + whole,
            out_specs=[out, out],
            out_shape=[jax.ShapeDtypeStruct((D, total), BF16)] * 2,
            **params,
        )(*lefts, *rights)

    steps = D // 2 // step
    half = steps // 2

    def kernel(*refs):
        upper, lower, right = refs[:size], refs[size : 2 * size], refs[2 * size : 3 * size]
        to_q, to_x, beside_top, below_low, keep = refs[3 * size :]

        @pl.when(pl.program_id(0) < half)
        def _():
            products(upper, right, keep, beside_top)
            products(lower, right, to_q.at[1], to_q.at[0])

        @pl.when(pl.program_id(0) >= half)
        def _():
            products(upper, right, keep, to_x.at[1])
            products(lower, right, below_low, to_x.at[0])

    first = lambda i: jnp.minimum(i, half - 1)
    last = lambda i: jnp.maximum(i - half, 0)
    rows = D // 4
    return pl.pallas_call(
        kernel,
        grid=(steps,),
        in_specs=[pl.BlockSpec((count, step), lambda i: (0, i))] * size
        + [pl.BlockSpec((count, step), lambda i: (0, i + steps))] * size
        + whole,
        out_specs=[
            pl.BlockSpec((2, step, total), lambda i: (0, first(i), 0)),
            pl.BlockSpec((2, step, total), lambda i: (0, last(i), 0)),
            pl.BlockSpec((step, total), lambda i: (first(i), 0)),
            pl.BlockSpec((step, total), lambda i: (last(i), 0)),
            pl.BlockSpec((step, total), lambda i: (i, 0)),
        ],
        out_shape=[
            jax.ShapeDtypeStruct(shape, BF16)
            for shape in (
                (2, rows, total), (2, rows, total), (rows, total), (rows, total), (2 * rows, total)
            )
        ],
        **params,
    )(*lefts, *lefts, *rights)


NN, NT, TN = ((1,), (0,)), ((1,), (1,)), ((0,), (0,))
VMEM_LIMIT = 60 << 20
LOCAL_BYTES = 200 << 20
HEADS_HERE = 2
ROWS = 2
LENGTH = 128
ROOT = HEAD_DIM ** (-0.5)


def mm(a, b, dims=NN):
    return lax.dot_general(a, b, (dims, ((), ())), preferred_element_type=F32)


def eye(size):
    return lax.broadcasted_iota(jnp.int32, (size, size), 0) == lax.broadcasted_iota(
        jnp.int32, (size, size), 1
    )


def to_column(row):
    return jnp.sum(jnp.where(eye(row.shape[1]), row, 0.0), axis=1, keepdims=True)


def to_row(column):
    return jnp.sum(jnp.where(eye(column.shape[0]), column, 0.0), axis=0, keepdims=True)


def head(values, kind, number):
    start = (number * 3 + kind) * HEAD_DIM
    return values[:, start : start + HEAD_DIM]


def pair(values, number):
    return values[:, number * HEAD_DIM : (number + 1) * HEAD_DIM]


def rotated(values, cosine, sine):
    return values * cosine + pltpu.roll(values, HEAD_DIM // 2, 1) * sine


def allowed_keys(segment_row):
    size = segment_row.shape[1]
    same = to_column(segment_row) == segment_row
    later = lax.broadcasted_iota(jnp.int32, (size, size), 1) > lax.broadcasted_iota(
        jnp.int32, (size, size), 0
    )
    return jnp.logical_and(same, jnp.logical_not(later))


def softmax_of(query, key, allowed):
    scores = jnp.where(allowed, mm(query, key, NT) * ROOT, -1e30)
    expo = jnp.exp(scores - jnp.max(scores, axis=1, keepdims=True))
    return expo / jnp.sum(expo, axis=1, keepdims=True)


def scale_of(squares, kind):
    return to_column(lax.rsqrt(squares[kind : kind + 1] / D + EPSILON))


def row_call(kernel, rows, ins, outs):
    def spec(shape, block):
        if block == "whole":
            return pl.BlockSpec(shape, lambda i: (0,) * len(shape))
        return pl.BlockSpec((ROWS * block,) + shape[1:], lambda i: (i,) + (0,) * (len(shape) - 1))

    return pl.pallas_call(
        kernel,
        grid=(rows // ROWS,),
        in_specs=[spec(v.shape, block) for v, block in ins],
        out_specs=[spec(shape, block) for shape, _, block in outs],
        out_shape=[jax.ShapeDtypeStruct(shape, dtype) for shape, dtype, _ in outs],
        compiler_params=pltpu.CompilerParams(vmem_limit_bytes=VMEM_LIMIT),
        cost_estimate=pl.CostEstimate(flops=0, bytes_accessed=0, transcendentals=0),
    )(*[v for v, _ in ins])


def row_views(row, *refs):
    return [ref.at[row * LENGTH : (row + 1) * LENGTH] for ref in refs]


def project_kernel(tokens, weights, out, squares):
    out[...] = mm(tokens[...], weights[...])
    for row in range(ROWS):
        [product] = row_views(row, out)
        for kind in range(2):
            total = 0.0
            for number in range(HEADS_HERE):
                part = head(product, kind, number)
                total = total + jnp.sum(part * part, axis=1, keepdims=True)
            squares[row, kind : kind + 1] = to_row(total)


def attend_kernel(
    qkv_all, squares, gains, cosine_all, sine_all, segments, weights,
    query_all, key_all, value_all, mixed_all, out,
):
    for row in range(ROWS):
        qkv, cosine, sine, query_out, key_out, value_out, mixed = row_views(
            row, qkv_all, cosine_all, sine_all, query_all, key_all, value_all, mixed_all
        )
        allowed = allowed_keys(segments[row])
        scales = [scale_of(squares[row], kind) for kind in range(2)]
        for number in range(HEADS_HERE):
            low = [
                rotated(
                    head(qkv, kind, number) * scales[kind] * gains[kind, number : number + 1],
                    cosine[...],
                    sine[...],
                ).astype(BF16)
                for kind in range(2)
            ]
            value = head(qkv, 2, number).astype(BF16)
            probs = softmax_of(*low, allowed).astype(BF16)
            where = slice(number * HEAD_DIM, (number + 1) * HEAD_DIM)
            query_out[:, where] = low[0]
            key_out[:, where] = low[1]
            value_out[:, where] = value
            mixed[:, where] = mm(probs, value).astype(BF16)
    out[...] = mm(mixed_all[...], weights[...], NT).astype(BF16)


def attend_back_kernel(
    grads, weights, query_all, key_all, value_all, qkv_all, squares, gains, cosine_all, sine_all,
    segments, weighted_all, value_grad_all, inner, gain_grad,
):
    @pl.when(pl.program_id(0) == 0)
    def _():
        gain_grad[...] = jnp.zeros_like(gain_grad)

    mixed_grads = mm(grads[...], weights[...]).astype(BF16)
    for row in range(ROWS):
        queries, keys, values, qkv, cosine, sine, weighted, value_grad = row_views(
            row, query_all, key_all, value_all, qkv_all, cosine_all, sine_all, weighted_all,
            value_grad_all,
        )
        allowed = allowed_keys(segments[row])
        scales = [scale_of(squares[row], kind) for kind in range(2)]
        sums = [0.0, 0.0]
        for number in range(HEADS_HERE):
            query, key, value = pair(queries, number), pair(keys, number), pair(values, number)
            mixed_grad = pair(mixed_grads[row * LENGTH : (row + 1) * LENGTH], number)
            probs = softmax_of(query, key, allowed)
            where = slice(number * HEAD_DIM, (number + 1) * HEAD_DIM)
            value_grad[:, where] = mm(probs.astype(BF16), mixed_grad, TN).astype(BF16)
            prob_grad = mm(mixed_grad, value, NT)
            score_grad = probs * (prob_grad - jnp.sum(probs * prob_grad, axis=1, keepdims=True))
            score_low = (score_grad * ROOT).astype(BF16)
            turned = (mm(score_low, key), mm(score_low, query, TN))
            for kind in range(2):
                normed = rotated(turned[kind], cosine[...], -sine[...])
                part = head(qkv, kind, number)
                gain_grad[kind, number : number + 1] += jnp.sum(
                    normed * part * scales[kind], axis=0, keepdims=True
                )
                normed = normed * gains[kind, number : number + 1]
                sums[kind] = sums[kind] + jnp.sum(part * normed, axis=1, keepdims=True)
                start = (kind * HEADS_HERE + number) * HEAD_DIM
                weighted[:, start : start + HEAD_DIM] = normed
        for kind in range(2):
            inner[row, kind : kind + 1] = to_row(sums[kind])


def input_grad_kernel(
    weighted_all, qkv_all, squares, inner, value_grad_all, weights, qkv_grad_all, out
):
    for row in range(ROWS):
        weighted, qkv, value_grad, qkv_grad = row_views(
            row, weighted_all, qkv_all, value_grad_all, qkv_grad_all
        )
        for kind in range(2):
            scale = scale_of(squares[row], kind)
            shift_by = scale * scale * scale * (to_column(inner[row][kind : kind + 1]) / D)
            for number in range(HEADS_HERE):
                start = (kind * HEADS_HERE + number) * HEAD_DIM
                part = weighted[:, start : start + HEAD_DIM]
                start = (number * 3 + kind) * HEAD_DIM
                qkv_grad[:, start : start + HEAD_DIM] = (
                    scale * part - head(qkv, kind, number) * shift_by
                ).astype(BF16)
        for number in range(HEADS_HERE):
            start = (number * 3 + 2) * HEAD_DIM
            qkv_grad[:, start : start + HEAD_DIM] = pair(value_grad, number)
    out[...] = mm(qkv_grad_all[...], weights[...], NT).astype(BF16)


class Place:
    def __init__(self, reps):
        self.reps = reps
        self.g = lax.axis_index("g")
        self.q = lax.axis_index("q")
        self.c = lax.axis_index("c")
        self.x = lax.axis_index("x")

    def orders(self):
        return [
            [
                (g * self.reps + (q ^ flip)) * CORES + c
                for q in range(self.reps)
                for c in range(CORES)
                for g in range(GROUP)
            ]
            for flip in ((0, 1) if self.reps == 2 else (0,))
        ]

    def shuffle(self, value, orders):
        if self.reps == 2:
            return reorder(value, self.q, orders)
        rows, size = value.shape[0], D // len(orders[0])
        blocks = value.reshape(rows, -1, size)
        return jnp.stack([blocks[:, i] for i in orders[0]], 1).reshape(rows, D)

    def to_local(self, value):
        return self.shuffle(value, self.orders())

    def to_global(self, value):
        return self.shuffle(
            value, [[order.index(i) for i in range(len(order))] for order in self.orders()]
        )

    def send(self, pieces):
        return [pieces[0]] + [shift(pieces[by], by) for by in range(1, GROUP)]

    def spread(self, shards):
        return self.send(pack(shards, self.g))

    def settle(self, pieces):
        mine, other = sort(pieces, self.g, self.c)
        return [mine, swap(other, "c")]

    def settled(self, halves):
        return by_core(*halves, self.c)

    def widen(self, held):
        if self.reps != 2:
            return [lax.all_gather(held, "q", axis=0, tiled=True)]
        return [held, swap(held, "q"), swap(held, "x")]

    def widened(self, blocks):
        if self.reps != 2:
            return [*blocks, swap(blocks[0], "x")]
        half = blocks[0].shape[0] // 2
        return [*blocks, swap(blocks[2][:half], "q"), swap(blocks[1][half:], "x")]

    def join(self, blocks, cuts):
        rows = blocks[0].shape[0]
        spots = [(0, 0), (0, 1)]
        if self.reps == 2:
            spots = [(0, 0), (rows, 0), (0, 1), (rows, 1), (rows + rows // 2, 1)]
        moves, shapes = [], [(D, 2 * (stop - start)) for start, stop in cuts]
        for number, (start, stop) in enumerate(cuts):
            for at, (row, side) in enumerate(spots):
                moves.append((at, (start, stop), number, row, side * (stop - start)))
        return assemble(blocks, moves, shapes)

    def narrow(self, parts):
        if self.reps != 2:
            return [swap(parts[1], "x")]
        return [swap(parts[0], "q"), swap(parts[1], "x")]

    def narrow_next(self, parts, came):
        if self.reps != 2:
            total = add(parts[0], came[0])
            return [lax.psum_scatter(total, "q", scatter_dimension=0, tiled=True)]
        _, _, beside_top, below_low, _ = parts
        return [swap(add(beside_top, came[0][0]), "x"), swap(add(below_low, came[1][0]), "q")]

    def narrowed(self, parts, came, more):
        if self.reps != 2:
            return jnp.split(more[0], 2)
        half = parts[4].shape[0] // 2
        return (
            add(parts[4][:half], more[0], came[0][1]),
            add(parts[4][half:], came[1][1], more[1]),
        )

    def unsettle(self, halves):
        top, low = halves
        mine, other = jnp.where(self.c == 0, top, low), jnp.where(self.c == 0, low, top)
        return [mine, swap(other, "c")]

    def collect(self, halves):
        return self.send(deal(*halves, self.g, self.c))


def rope_tables(segments):
    places = jnp.arange(segments.shape[1], dtype=jnp.int32)
    same = segments[:, :, None] == segments[:, None, :]
    earlier = same & (places[None, None, :] < places[None, :, None])
    spot = jnp.sum(earlier.astype(jnp.int32), axis=2).astype(F32)
    halfway = HEAD_DIM // 2
    inverse = jnp.exp(jnp.arange(halfway, dtype=F32) * (-2.0 * math.log(ROPE_BASE) / HEAD_DIM))
    angles = spot.reshape(-1, 1) * inverse
    cosine, sine = jnp.cos(angles), jnp.sin(angles)
    return jnp.concatenate([cosine, cosine], 1), jnp.concatenate([-sine, sine], 1)


def norm_scale(values):
    return lax.rsqrt(jnp.mean(values * values, axis=-1, keepdims=True) + EPSILON)


def norm_back(values, scale, gain, grad):
    weighted = grad * gain
    inner = jnp.sum(values * weighted, axis=-1, keepdims=True) / D
    return (
        scale * weighted - values * (scale * scale * scale) * inner,
        jnp.sum(grad * values * scale, axis=0),
    )


def on_device(
    reps,
    tokens,
    segment_ids,
    query_proj,
    key_proj,
    value_proj,
    out_proj,
    query_gain,
    key_gain,
    attn_gain,
    gate_proj,
    up_proj,
    down_proj,
    mlp_gain,
    cotangent,
):
    place = Place(reps)
    slots = GROUP * CORES
    shard_rows = query_proj.shape[0]
    length = tokens.shape[2]
    slot = place.g * CORES + place.c

    step = Order()
    count = slots * length
    cut = 3 * HEAD_DIM

    def team_scatter(value):
        return lax.psum_scatter(value, TEAM, scatter_dimension=0, tiled=True)

    def team_gather(value):
        return lax.all_gather(value, TEAM, axis=0, tiled=True)

    def team_sum(value):
        value = value + step(swap(value, "c"))
        for by in (1, 2):
            value = value + step(
                lax.ppermute(value, "g", [(i, i ^ by) for i in range(GROUP)])
            )
        return value

    attn = place.spread([query_proj, key_proj, value_proj, out_proj])
    own_row = place.to_local(pick(tokens, place.x, 0)[0])
    segments = pick(segment_ids, place.x, 0)
    segments = ordered(place.c, segments, swap(segments, "c"), 0)[:, 0]
    gate = pack([gate_proj], place.g)
    feed = pack([up_proj, down_proj], place.g)
    attn, own_row, segments, gate, feed = step(attn, own_row, segments, gate, feed)
    all_rows = team_gather(own_row)
    segments = [segments] + [shift(segments, by) for by in range(1, GROUP)]
    attn = step(place.settle(attn))
    attn = place.widen(place.settled(attn))
    gains = jnp.stack([pick(w.reshape(slots, HEAD_DIM), slot, 0) for w in (query_gain, key_gain)])
    gains = jnp.stack([gains, swap(gains, "x")], 1)
    gathered = jnp.zeros((GROUP,) + segments[0].shape, segments[0].dtype)
    for by, piece in enumerate(segments):
        gathered = put(gathered, piece, (place.g - by) % GROUP)
    segments = gathered.reshape(slots, length)
    cosine, sine = rope_tables(segments)
    segments = segments.astype(F32)[:, None]
    attn, gains, segments, gate = step(attn, gains, segments, gate)
    gate = place.send(gate)
    attn = step(place.widened(attn))
    qkv_full, out_full = step(place.join(attn, [(0, cut), (cut, 4 * HEAD_DIM)]))
    all_rows, cosine, sine = step(all_rows, cosine, sine)

    qkv, squares = step(
        *row_call(
            project_kernel,
            slots,
            [(all_rows, length), (qkv_full, "whole")],
            [((count, 6 * HEAD_DIM), F32, length), ((slots, 2, length), F32, 1)],
        )
    )
    gate = step(place.settle(step(gate)))
    gate = place.widen(place.settled(gate))
    squares = team_sum(squares)
    squares, feed = step(squares, feed)
    feed = place.send(feed)
    low = ((count, 2 * HEAD_DIM), BF16, length)
    query_low, key_low, value_low, mixed, attn_part, gate = step(
        *row_call(
            attend_kernel,
            slots,
            [
                (qkv, length),
                (squares, 1),
                (gains, "whole"),
                (cosine, length),
                (sine, length),
                (segments, 1),
                (out_full, "whole"),
            ],
            [low, low, low, low, ((count, D), BF16, length)],
        ),
        gate,
    )
    gate = place.widened(gate)
    attn_part, gate, feed = step(attn_part, gate, feed)
    projected = team_scatter(attn_part)
    feed = place.settle(feed)
    feed = place.widen(place.settled(step(feed)))
    width = gate_proj.shape[1] // slots
    feed = step(feed)
    projected = step(projected)
    projected = projected.astype(F32)
    attn_gain, mlp_gain = place.to_local(jnp.stack([attn_gain, mlp_gain]))
    projected_scale = norm_scale(projected)
    hidden = own_row.astype(F32) + projected * projected_scale * attn_gain
    hidden_low, hidden = step(hidden.astype(BF16), hidden)
    hidden_all = team_gather(hidden_low)
    [gate_full] = step(place.join(gate, [(0, width)]))
    feed = place.widened(feed)
    up_full, down_full = place.join(step(feed), [(0, width), (width, 2 * width)])
    own_cotangent = place.to_local(pick(cotangent, place.x, 0)[0]).astype(F32)
    hidden_all, gate_full, up_full, down_full, own_cotangent = step(
        hidden_all, gate_full, up_full, down_full, own_cotangent
    )

    lifted = dot(hidden_all, up_full)
    gated = dot(hidden_all, gate_full)
    active = (gated / (1.0 + jnp.exp(-gated)) * lifted).astype(BF16)
    reduced = team_scatter(step(dot_nt(active, down_full).astype(BF16)))
    reduced = step(reduced).astype(F32)
    reduced_scale = norm_scale(reduced)
    reduced_grad, mlp_gain_grad = norm_back(reduced, reduced_scale, mlp_gain, own_cotangent)
    reduced_all = team_gather(step(reduced_grad.astype(BF16)))
    own_out = place.to_global((hidden + reduced * reduced_scale * mlp_gain).astype(BF16))
    layer_out = ordered(place.x, own_out, swap(own_out, "x"), 0)[:, None]
    reduced_all, mlp_gain_grad, layer_out = step(reduced_all, mlp_gain_grad, layer_out)

    active_grad = dot(reduced_all, down_full)
    gate_sigmoid = 1.0 / (1.0 + jnp.exp(-gated))
    gated_grad = (
        active_grad * lifted * gate_sigmoid * (1.0 + gated * (1.0 - gate_sigmoid))
    ).astype(BF16)
    lifted_grad = (active_grad * gated * gate_sigmoid).astype(BF16)
    hidden_part = dot_nt(gated_grad, gate_full) + dot_nt(lifted_grad, up_full)
    hidden_part, gated_grad, lifted_grad = step(hidden_part.astype(BF16), gated_grad, lifted_grad)
    hidden_part = team_scatter(hidden_part)
    down = step(weight_grads([(reduced_all, active)], reps, [width]))
    down_came = place.narrow(down)
    feed = step(
        weight_grads([(hidden_all, gated_grad), (hidden_all, lifted_grad)], reps, [width, width])
    )
    down_came = step(down_came)
    down_more = place.narrow_next(down, down_came)
    hidden_grad = own_cotangent + step(hidden_part).astype(F32)
    projected_grad, attn_gain_grad = norm_back(projected, projected_scale, attn_gain, hidden_grad)
    projected_low, hidden_grad, attn_gain_grad = step(
        projected_grad.astype(BF16), hidden_grad, attn_gain_grad
    )
    projected_all = team_gather(projected_low)
    down_more, feed = step(down_more, feed)
    feed_came = place.narrow(feed)
    down = step(place.unsettle(place.narrowed(down, down_came, down_more)))
    norm_gain_grads = place.to_global(jnp.stack([attn_gain_grad, mlp_gain_grad]))
    down = deal(*down, place.g, place.c)
    norm_gain_grads, down = step(norm_gain_grads, down)

    projected_all, down = step(projected_all, down)
    down = place.send(down)
    weighted, value_grad, inner, head_gain_grads, down, feed_came = step(
        *row_call(
            attend_back_kernel,
            slots,
            [
                (projected_all, length),
                (out_full, "whole"),
                (query_low, length),
                (key_low, length),
                (value_low, length),
                (qkv, length),
                (squares, 1),
                (gains, "whole"),
                (cosine, length),
                (sine, length),
                (segments, 1),
            ],
            [
                ((count, 4 * HEAD_DIM), F32, length),
                low,
                ((slots, 2, length), F32, 1),
                (gains.shape, F32, "whole"),
            ],
        ),
        down,
        feed_came,
    )
    spots = jnp.zeros((2, 2, slots, HEAD_DIM), F32)
    for number in range(2):
        spots = lax.dynamic_update_slice(
            spots,
            head_gain_grads[:, number][:, None, None],
            (0, place.x if number == 0 else 1 - place.x, slot, 0),
        )
    message = jnp.concatenate([v.reshape(-1, HEAD_DIM) for v in (inner, spots, norm_gain_grads)])
    feed_more = place.narrow_next(feed, feed_came)
    message = team_sum(message)
    inner, gain_grads = message[: 2 * slots].reshape(inner.shape), message[2 * slots :]
    gain_x = swap(gain_grads, "x")
    qkv_grad, input_part, feed_more, gain_x = step(
        *row_call(
            input_grad_kernel,
            slots,
            [
                (weighted, length),
                (qkv, length),
                (squares, 1),
                (inner, 1),
                (value_grad, length),
                (qkv_full, "whole"),
            ],
            [((count, 6 * HEAD_DIM), BF16, length), ((count, D), BF16, length)],
        ),
        feed_more,
        gain_x,
    )
    input_part = team_scatter(input_part)
    feed = step(place.unsettle(place.narrowed(feed, feed_came, feed_more)))
    qkv_grad, feed = step(qkv_grad, deal(*feed, place.g, place.c))
    feed = place.send(feed)
    attn, feed[1] = step(
        weight_grads([(all_rows, qkv_grad), (projected_all, mixed)], reps, [cut, HEAD_DIM]),
        feed[1],
    )
    attn_came = place.narrow(attn)
    gain_grads = gain_grads + gain_x
    gain_q = swap(gain_grads, "q") if reps == 2 else lax.psum(gain_grads, "q") - gain_grads
    [down_grad] = step(unpack(down, place.g, 1))
    attn_came = step(attn_came)
    attn_more = place.narrow_next(attn, attn_came)
    input_part = step(input_part)
    own_grad = place.to_global((hidden_grad + input_part.astype(F32)).astype(BF16))
    own_grad_x = swap(step(own_grad), "x")
    feed = step(feed)
    attn_more = step(attn_more)
    attn = place.unsettle(place.narrowed(attn, attn_came, attn_more))
    attn, gain_q = step(attn, gain_q)
    attn = place.send(step(deal(*attn, place.g, place.c)))
    attn[1], feed, own_grad_x = step(attn[1], feed, own_grad_x)
    gate_grad, up_grad = unpack(feed, place.g, 2)
    summed = (gain_grads + gain_q).reshape(4, D)
    tokens_grad = ordered(place.x, own_grad, own_grad_x, 0)[:, None].astype(F32)
    tokens_grad, gate_grad, up_grad, summed = step(tokens_grad, gate_grad, up_grad, summed)
    attn_grads = unpack(step(attn), place.g, 4)
    summed = summed + step.token
    half_of = lambda v: pick(v.reshape(2, -1), place.x, 0)
    return (
        layer_out,
        tokens_grad,
        *attn_grads,
        half_of(summed[0]),
        half_of(summed[1]),
        summed[2],
        gate_grad,
        up_grad,
        down_grad,
        summed[3],
    )


def solution(mesh):
    reps = mesh.shape["dp"] // (GROUP * CORES)
    folded = Mesh(
        mesh.devices.reshape(GROUP, reps, CORES, mesh.shape["tensor"]), ("g", "q", "c", "x")
    )
    dp = ("g", "q", "c")
    row = P(None, dp, None, None)
    weight = P(dp, "x")
    gain = P("x")
    in_specs = (row, P(None, dp, None)) + (weight,) * 4 + (gain, gain, P()) + (weight,) * 3
    in_specs += (P(), row)
    out_specs = (row, row) + (weight,) * 4 + (gain, gain, P()) + (weight,) * 3 + (P(),)

    def body(*args):
        return on_device(reps, *args)

    return jax.shard_map(
        body, mesh=folded, in_specs=in_specs, out_specs=out_specs, check_vma=False
    )
```
